128 devices in a mesh: fluid: 8 (over z, core), patch: 16 (over x, y).
Axes of the slice: x: 4, y: 4, z: 4, core: 2. Of those that a mesh axis runs over, the one named last changes fastest.
Arguments:
- contributions: bfloat16 [262144, 256], P(('fluid', 'patch')), may hold values from -6 to 6
- routes: int32 [262144, 1], P(('fluid', 'patch')), may hold values from 0 to 127; in each aligned block of 2048 rows (0 to 2047, 2048 to 4095, ...) at most 32 rows name the same one
- slots: int32 [262144], P(('fluid', 'patch')), may hold values from 0 to 767
- panels: bfloat16 [98304, 12288], P(('fluid', 'patch')), may hold values from -0.0546875 to 0.0546875
Outputs:
- traces: bfloat16 [98304, 256], P(('fluid', 'patch'))
- added_mass: float32 [256, 256], replicated
The draws below stay inside these ranges and needn't reach their ends.
Inputs may be any that keep to these rules, and one draw needn't show every extreme that they name: `routes`: among the rows of one device, at most 32 name the same owner.
All inputs are finite; a program needn't handle non-finite values.
Results may differ from the reference program's by a relative error of at most 0.0051.
Values may be sent and summed in bfloat16 or wider, within the bound.
A program may use at most 128 MiB of HBM per device.

```python
import math
import jax
import jax.numpy as jnp
import numpy as np
from jax import lax

COLS = 256
NODE_DEV = 768
TR_DEV = 2048
CAP = 32
GROUP_ROWS = 12288
NODES = 98304
TRACES = 262144
N_FLUID = 8
DEVICES = 128


def place_ends(values, key, low, largest):
    shape = values.shape
    index_at = [jax.random.randint(jax.random.fold_in(key, axis), (), 0, shape[axis]) for axis in range(len(shape))]
    values = values.at[tuple(index_at)].set(low)
    longest = shape.index(max(shape))
    index_at[longest] = (index_at[longest] + 1) % shape[longest]
    return values.at[tuple(index_at)].set(largest)


def levels(rng, extent, shards, smallest, high):
    def one(dim, shards_of):
        steps = jax.random.uniform(jax.random.fold_in(jax.random.fold_in(rng, 6), dim), (shards_of,), jnp.float32, smallest / len(shards), high / len(shards))
        return jnp.repeat(jnp.exp(steps), extent[dim] // shards_of).reshape((-1,) + (1,) * (len(extent) - dim - 1))

    factor_of = one(*shards[0])
    for cut in shards[1:]:
        factor_of = factor_of * one(*cut)
    return factor_of


def routed_block(rng, own, number, rows, amount, top, limit, skew):
    ranking = jax.random.permutation(rng, amount)
    heavy_load, ordinary = load_shares(amount, rows * top, limit, skew, True), load_shares(amount, rows * top, limit, skew, False)
    places = jnp.arange(amount)

    def named(tallies, rotation):
        used = int((tallies > 0).sum())
        fixed = max(1, used // 4)
        shifted = fixed + (places - fixed + rotation * (used - fixed)) % max(1, amount - fixed)
        return jnp.zeros((amount,), jnp.int32).at[ranking[jnp.where(places < fixed, places, shifted)]].set(jnp.asarray(tallies, jnp.int32))

    tallies = jnp.where(number % 4 == 0, named(heavy_load, number // 4), named(ordinary, number - number // 4 - 1))
    mixed = jax.random.permutation(jax.random.fold_in(own, 3), amount)
    source_of, receiver = mixed[0:amount // 2 * 2:2], mixed[1:amount // 2 * 2:2]
    margin = jnp.minimum(tallies[source_of] - 1, limit - tallies[receiver]) // 2
    margin = jnp.where((source_of == ranking[0]) | (receiver == ranking[0]) | (tallies[receiver] == 0), 0, jnp.maximum(margin, 0))
    shifted = jax.random.randint(jax.random.fold_in(own, 4), (amount // 2,), 0, 1 << 20) % (margin + 1)
    tallies = tallies.at[source_of].add(-shifted).at[receiver].add(shifted)
    members = jnp.searchsorted(jnp.cumsum(tallies), jnp.arange(rows * top), side="right").astype(jnp.int32)
    table = members.reshape(top, rows).T
    table = table[jax.random.permutation(jax.random.fold_in(own, 1), rows)]
    rotation = jax.random.randint(jax.random.fold_in(own, 2), (rows, 1), 0, top)
    return jnp.take_along_axis(table, (jnp.arange(top)[None, :] + rotation) % top, axis=1)


def load_shares(number_of, total, limit, lean, full):
    loads = [(1 << 20) // math.isqrt(standing ** lean) + 1 for standing in range(1, number_of + 1)]
    largest = limit if full else min(limit, max(-(-total // number_of), total * loads[0] // sum(loads)))
    least = 1 if total - largest >= number_of - 1 else 0
    holding, surplus = [largest] + [least] * (number_of - 1), total - largest - least * (number_of - 1)
    while surplus > 0:
        candidates = [i for i in range(1, number_of) if holding[i] < largest] or [i for i in range(1, number_of) if holding[i] < limit]
        pool, remaining = sum([loads[i] for i in candidates]), surplus
        for i in candidates:
            addition = min(limit - holding[i], max(1, remaining * loads[i] // pool), surplus)
            holding[i] = holding[i] + addition
            surplus = surplus - addition
    return np.array(holding)


def noise(rng, dims, width, reach, pieces=(), dtype=jnp.bfloat16):
    values = jax.random.normal(rng, dims, jnp.float32) * width
    if len(pieces) > 0:
        values = levels(rng, dims, pieces, -0.22, 0.18) * values
    return jnp.clip(values, min=-reach, max=reach).astype(dtype)


def setup_inputs(seed: int = 0) -> dict:
    keys = jax.random.split(jax.random.key(seed), 5)
    contributions = noise(keys[0], (TRACES, COLS), 1.0, 6.0, ((0, 128),))
    routes_keys = jax.random.split(jax.random.fold_in(keys[1], 1), TRACES // TR_DEV)
    routes_turns = jax.random.permutation(jax.random.fold_in(keys[1], 3), TRACES // TR_DEV)
    routes = jax.vmap(lambda own, number: routed_block(jax.random.fold_in(keys[1], 2), own, number, TR_DEV, DEVICES, 1, CAP, 2))(routes_keys, routes_turns).reshape((TRACES, 1))
    slots = place_ends(jax.random.randint(keys[2], (TRACES,), 0, NODE_DEV), jax.random.fold_in(keys[2], 1), 0, NODE_DEV - 1).astype(jnp.int32)
    panels = noise(keys[3], (NODES, GROUP_ROWS), GROUP_ROWS ** -0.5, 0.0546875, ((0, 128),))
    return {"contributions": contributions, "routes": routes, "slots": slots, "panels": panels}


def coupling_of(member_pair):
    traces_group, panel_group = member_pair
    coupled = jnp.dot(panel_group, traces_group, preferred_element_type=jnp.float32)
    return jnp.dot(traces_group.astype(jnp.float32).T, coupled, precision=lax.Precision.HIGHEST)

def reference(contributions, routes, slots, panels):
    node_ids = (routes[:, 0] * NODE_DEV + slots).astype(jnp.int32)
    traces = jax.ops.segment_sum(contributions.astype(jnp.float32), node_ids, num_segments=NODES).astype(jnp.bfloat16)
    grouped = traces.reshape(N_FLUID, GROUP_ROWS, COLS)
    panel_groups = panels.reshape(N_FLUID, GROUP_ROWS, GROUP_ROWS)
    partials = lax.map(coupling_of, (grouped, panel_groups))
    summed_mass = lax.optimization_barrier(jnp.sum(partials, axis=0))
    added_mass = (summed_mass + summed_mass.T) * (0.5 / math.sqrt(NODES))
    return (traces, added_mass)
```

```python
import functools
import math

import jax
import jax.numpy as jnp
from jax import lax
from jax.experimental import pallas as pl
from jax.experimental.pallas import tpu as pltpu
from jax.sharding import PartitionSpec as P

MESH = pl.DeviceIdType.MESH
SIDE = 4
COLUMN = 8
PLANE = 16
CAP = 32
STRIDE = 5


def where_am_i():
    f, p = lax.axis_index("fluid"), lax.axis_index("patch")
    return f // 2, lax.rem(f, 2), p // SIDE, lax.rem(p, SIDE)


def shifted(column_step, plane_step, sign=1):
    z, c, x, y = where_am_i()
    dz, dc = column_step // 2, column_step % 2
    dx, dy = plane_step // SIDE, plane_step % SIDE
    if sign < 0:
        dz, dx, dy = SIDE - dz, SIDE - dx, SIDE - dy
    return (
        lax.rem(z + dz, SIDE) * 2 + lax.rem(c + dc, 2),
        lax.rem(x + dx, SIDE) * SIDE + lax.rem(y + dy, SIDE),
    )


def kernel(
    factor, contributions, routes, slots, panels, traces, mass,
    out_rows, in_rows, onehot, position, slot_out, column_slots, plane_out, plane_slots, landed,
    gathered, panel_v, coupled, share, reduce_in, column_in, full,
    row_send, row_recv, slot_send, slot_recv, plane_send, plane_recv, gather_send, gather_recv, panel_sem,
    reduce_send, reduce_recv, column_send, column_recv, full_send, full_recv,
):
    f32, bf16, i32 = jnp.float32, jnp.bfloat16, jnp.int32
    f, p = lax.axis_index("fluid"), lax.axis_index("patch")
    z, c, x, y = where_am_i()
    rows = contributions.shape[0]
    nodes = traces.shape[0]
    width = traces.shape[1]
    half, piece = nodes // 2, nodes // 4

    barrier = pltpu.get_barrier_semaphore()

    @pl.loop(1, COLUMN * PLANE)
    def _(i):
        pl.semaphore_signal(barrier, inc=1, device_id=shifted(i // PLANE, i % PLANE), device_id_type=MESH)

    panel_copies = []
    for s in range(PLANE):
        dx, dy = s // SIDE, s % SIDE
        owner = lax.rem(x + SIDE - dx, SIDE) * SIDE + lax.rem(y + SIDE - dy, SIDE)
        copy = pltpu.make_async_copy(
            panels.at[:, pl.ds(pl.multiple_of(owner * nodes, 128), nodes)], panel_v.at[s], panel_sem.at[s]
        )
        copy.start()
        panel_copies.append(copy)

    to = routes[...]
    to_f, to_p = to >> 4, to & 15
    dz, dc = ((to_f >> 1) - z) & 3, ((to_f & 1) - c) & 1
    dx, dy = ((to_p >> 2) - x) & 3, ((to_p & 3) - y) & 3
    step_column, step_plane = dz * 2 + dc, dx * 4 + dy
    label = step_column * PLANE + step_plane
    onehot[...] = (lax.broadcasted_iota(i32, (128, rows), 0) == label).astype(bf16)
    block = 256
    upper = (
        lax.broadcasted_iota(i32, (block, block), 0) < lax.broadcasted_iota(i32, (block, block), 1)
    ).astype(bf16)
    seen = jnp.zeros((128, 1), f32)
    orders = []
    for b in range(rows // block):
        mine = onehot[:, b * block:(b + 1) * block]
        before = jnp.dot(mine, upper, preferred_element_type=f32) + seen
        wide = mine.astype(f32)
        orders.append(jnp.sum(wide * before, axis=0, keepdims=True))
        seen = seen + jnp.sum(wide, axis=1, keepdims=True)
    order = jnp.concatenate(orders, axis=1).astype(i32)
    turn = (step_plane - STRIDE * step_column) & 15
    position[...] = (turn * COLUMN + step_column) * CAP + order

    value = slots[...] + 1
    lane_order = lax.broadcasted_iota(i32, (128, rows), 0) & (CAP - 1)
    hit = lane_order == order
    nt = (((1,), (1,)), ((), ()))
    high = jnp.where(hit, (value >> 5).astype(f32), 0.0).astype(bf16)
    table = lax.dot_general(onehot[...], high, nt, preferred_element_type=f32) * 32.0
    low = jnp.where(hit, (value & 31).astype(f32), 0.0).astype(bf16)
    table = table + lax.dot_general(onehot[...], low, nt, preferred_element_type=f32)
    lane_group = lax.broadcasted_iota(i32, (128, 128), 1) >> 5
    row_group = (lax.broadcasted_iota(i32, (128, 128), 0) >> 4) & 3
    slot_out[...] = jnp.where(lane_group == row_group, table, 0.0).astype(i32)
    column_slots[0] = slot_out[0:PLANE]

    pl.semaphore_wait(barrier, COLUMN * PLANE - 1)

    slot_copies = []
    for w in range(1, COLUMN):
        copy = pltpu.make_async_remote_copy(
            src_ref=slot_out.at[pl.ds(w * PLANE, PLANE)], dst_ref=column_slots.at[w],
            send_sem=slot_send.at[w], recv_sem=slot_recv.at[w], device_id=shifted(w, 0), device_id_type=MESH,
        )
        copy.start()
        slot_copies.append(copy)

    def build(kk):
        i = lax.broadcasted_iota(i32, (256, 1), 0)
        pick = (kk * 256 + i == position[...]).astype(bf16)
        made = jnp.dot(pick, contributions[...], preferred_element_type=f32).astype(bf16)
        out_rows[pl.ds(pl.multiple_of(kk * 256, 256), 256), :] = made

    def row_copy(kk, w):
        at = pl.ds(pl.multiple_of(kk * 256 + w * CAP, CAP), CAP)
        return pltpu.make_async_remote_copy(
            src_ref=out_rows.at[at], dst_ref=in_rows.at[at],
            send_sem=row_send, recv_sem=row_recv.at[kk],
            device_id=shifted(w, lax.rem(kk + STRIDE * w, PLANE)), device_id_type=MESH,
        )

    @pl.loop(1, PLANE)
    def _(kk):
        build(kk)
        for w in range(COLUMN):
            row_copy(kk, w).start()

    build(0)
    for w in range(1, COLUMN):
        row_copy(0, w).start()
    in_rows[0:CAP, :] = out_rows[0:CAP, :]

    for copy in slot_copies:
        copy.wait()
    first = column_slots[0] + column_slots[1] + column_slots[2] + column_slots[3]
    second = column_slots[4] + column_slots[5] + column_slots[6] + column_slots[7]
    sub = lax.broadcasted_iota(i32, (PLANE, 8, 128), 1)
    plane_out[...] = jnp.where(sub < 4, first[:, None, :], second[:, None, :])
    plane_slots[0] = plane_out[0]
    plane_copies = []
    for s in range(1, PLANE):
        copy = pltpu.make_async_remote_copy(
            src_ref=plane_out.at[s], dst_ref=plane_slots.at[s],
            send_sem=plane_send.at[s], recv_sem=plane_recv.at[s], device_id=shifted(0, s), device_id_type=MESH,
        )
        copy.start()
        plane_copies.append(copy)
    for copy in plane_copies:
        copy.wait()

    landed[...] = jnp.zeros_like(landed)

    def land(kk):
        group = lax.broadcasted_iota(i32, (1, 128), 1) >> 5
        parts = []
        for side in range(2):
            row = jnp.zeros((1, 128), i32)
            for k in range(4):
                w = side * 4 + k
                got = plane_slots[lax.rem(kk + STRIDE * w, PLANE), pl.ds(side * 4, 1), :]
                row = row + jnp.where(group == k, got, 0)
            parts.append(row)
        names = jnp.concatenate(parts, axis=1) - 1
        spread = (lax.broadcasted_iota(i32, (nodes, 256), 0) == names).astype(bf16)
        landed[...] += jnp.dot(
            spread, in_rows[pl.ds(pl.multiple_of(kk * 256, 256), 256), :], preferred_element_type=f32
        )

    def arrival(kk, start, count):
        at = pl.ds(start, count)
        return pltpu.make_async_remote_copy(
            src_ref=in_rows.at[at], dst_ref=in_rows.at[at],
            send_sem=row_send, recv_sem=row_recv.at[kk], device_id=(f, p), device_id_type=MESH,
        )

    @pl.loop(1, PLANE)
    def _(kk):
        arrival(kk, pl.multiple_of(kk * 256, 256), 256).wait_recv()
        land(kk)

    arrival(0, CAP, 256 - CAP).wait_recv()
    land(0)
    own = landed[...].astype(bf16)
    gathered[0] = own

    sent = []

    def pass_on(axis, direction, source, start, count, sem):
        dx, dy = source
        if axis == 0:
            dx = (dx + direction) % SIDE
            device = (f, lax.rem(x + direction + SIDE, SIDE) * SIDE + y)
        else:
            dy = (dy + direction) % SIDE
            device = (f, x * SIDE + lax.rem(y + direction + SIDE, SIDE))
        at = pl.ds(start, count)
        copy = pltpu.make_async_remote_copy(
            src_ref=gathered.at[source[0] * SIDE + source[1], at], dst_ref=gathered.at[dx * SIDE + dy, at],
            send_sem=gather_send, recv_sem=gather_recv.at[(dx * SIDE + dy) * 4 + sem],
            device_id=device, device_id_type=MESH,
        )
        copy.start()
        sent.append(count)

    def await_piece(source, start, count, sem):
        s = source[0] * SIDE + source[1]
        at = pl.ds(start, count)
        pltpu.make_async_remote_copy(
            src_ref=gathered.at[s, at], dst_ref=gathered.at[s, at],
            send_sem=gather_send, recv_sem=gather_recv.at[s * 4 + sem], device_id=(f, p), device_id_type=MESH,
        ).wait_recv()

    def at(lead, a, b):
        return (a, b) if lead == 0 else (b, a)

    def send_half(lead, axis, direction, source):
        pass_on(axis, direction, source, lead * half, half, lead * 2)

    def send_piece(lead, axis, direction, source, k):
        pass_on(axis, direction, source, lead * half + k * piece, piece, lead * 2 + k)

    def wait_half(lead, source):
        await_piece(source, lead * half, half, lead * 2)

    def wait_piece(lead, source, k):
        await_piece(source, lead * half + k * piece, piece, lead * 2 + k)

    def multiply(s, start, count):
        coupled[...] += jnp.dot(
            panel_v[s, :, pl.ds(start, count)], gathered[s, pl.ds(start, count), :], preferred_element_type=f32
        )

    for lead in (0, 1):
        for direction in (1, -1):
            send_half(lead, lead, direction, (0, 0))
            send_half(lead, 1 - lead, direction, (0, 0))
    traces[...] = own
    coupled[...] = jnp.zeros_like(coupled)
    for copy in panel_copies:
        copy.wait()
    multiply(0, 0, nodes)

    def multiply_halves(places):
        for lead, place in places:
            multiply(place[0] * SIDE + place[1], lead * half, half)

    for k, a, direction in ((0, 1, 1), (1, 3, -1)):
        for lead in (0, 1):
            place = at(lead, a, 0)
            wait_half(lead, place)
            send_piece(lead, lead, direction, place, k)
            send_half(lead, 1 - lead, 1, place)
            send_half(lead, 1 - lead, -1, place)
    for k, b, direction in ((0, 1, 1), (1, 3, -1)):
        for lead in (0, 1):
            place = at(lead, 0, b)
            wait_half(lead, place)
            send_piece(lead, 1 - lead, direction, place, k)
    multiply_halves([(lead, at(lead, a, b)) for a, b in ((1, 0), (3, 0), (0, 1), (0, 3)) for lead in (0, 1)])
    for k in (0, 1):
        for lead in (0, 1):
            place = at(lead, 2, 0)
            wait_piece(lead, place, k)
            send_piece(lead, 1 - lead, 1, place, k)
            send_piece(lead, 1 - lead, -1, place, k)
    multiply_halves([(lead, at(lead, 2, 0)) for lead in (0, 1)])
    for a in (1, 3):
        for k, b, direction in ((0, 1, 1), (1, 3, -1)):
            for lead in (0, 1):
                place = at(lead, a, b)
                wait_half(lead, place)
                send_piece(lead, 1 - lead, direction, place, k)
        multiply_halves([(lead, at(lead, a, b)) for b in (1, 3) for lead in (0, 1)])
    for k in (0, 1):
        for lead in (0, 1):
            wait_piece(lead, at(lead, 0, 2), k)
    multiply_halves([(lead, at(lead, 0, 2)) for lead in (0, 1)])
    for lead in (0, 1):
        place = at(lead, 2, 1)
        wait_piece(lead, place, 0)
        send_piece(lead, 1 - lead, 1, place, 0)
        place = at(lead, 2, 3)
        wait_piece(lead, place, 1)
        send_piece(lead, 1 - lead, -1, place, 1)
    for lead in (0, 1):
        wait_piece(lead, at(lead, 2, 1), 1)
        wait_piece(lead, at(lead, 2, 3), 0)
    multiply_halves([(lead, at(lead, 2, b)) for b in (1, 3) for lead in (0, 1)])
    for a in (1, 3):
        for k in (0, 1):
            for lead in (0, 1):
                wait_piece(lead, at(lead, a, 2), k)
        multiply_halves([(lead, at(lead, a, 2)) for lead in (0, 1)])
    for k in (0, 1):
        for lead in (0, 1):
            wait_piece(lead, at(lead, 2, 2), k)
    multiply_halves([(lead, at(lead, 2, 2)) for lead in (0, 1)])

    tn = (((0,), (0,)), ((), ()))
    top = coupled[...].astype(bf16)
    rest = (coupled[...] - top.astype(f32)).astype(bf16)
    share[...] = lax.dot_general(own, top, tn, preferred_element_type=f32) + lax.dot_general(
        own, rest, tn, preferred_element_type=f32
    )

    strip = width // PLANE
    copies = []
    for s in range(1, PLANE):
        device = shifted(0, s)
        copy = pltpu.make_async_remote_copy(
            src_ref=share.at[pl.ds(pl.multiple_of(device[1] * strip, strip), strip)], dst_ref=reduce_in.at[s],
            send_sem=reduce_send.at[s], recv_sem=reduce_recv.at[s], device_id=device, device_id_type=MESH,
        )
        copy.start()
        copies.append(copy)
    total = share[pl.ds(pl.multiple_of(p * strip, strip), strip), :]
    for s, copy in enumerate(copies):
        copy.wait()
        total = total + reduce_in[s + 1]
    column_in[f] = total
    copies = []
    for w in range(1, COLUMN):
        copy = pltpu.make_async_remote_copy(
            src_ref=column_in.at[f], dst_ref=column_in.at[f],
            send_sem=column_send.at[w], recv_sem=column_recv.at[w], device_id=shifted(w, 0), device_id_type=MESH,
        )
        copy.start()
        copies.append(copy)
    for copy in copies:
        copy.wait()
    total = column_in[0]
    for w in range(1, COLUMN):
        total = total + column_in[w]
    mine = pl.ds(pl.multiple_of(p * strip, strip), strip)
    full[mine, :] = total
    copies = []
    for s in range(1, PLANE):
        copy = pltpu.make_async_remote_copy(
            src_ref=full.at[mine], dst_ref=full.at[mine],
            send_sem=full_send.at[s], recv_sem=full_recv.at[s], device_id=shifted(0, s), device_id_type=MESH,
        )
        copy.start()
        copies.append(copy)
    for copy in copies:
        copy.wait()
    mass[...] = (full[...] + full[...].T) * factor

    everything = pl.ds(CAP, rows * 2 - CAP)
    pltpu.make_async_remote_copy(
        src_ref=out_rows.at[everything], dst_ref=out_rows.at[everything],
        send_sem=row_send, recv_sem=row_recv.at[0], device_id=(f, p), device_id_type=MESH,
    ).wait_send()
    assert sum(sent) % nodes == 0
    blocks = pl.ds(0, sum(sent) // nodes)
    pltpu.make_async_remote_copy(
        src_ref=gathered.at[blocks], dst_ref=gathered.at[blocks],
        send_sem=gather_send, recv_sem=gather_recv.at[0], device_id=(f, p), device_id_type=MESH,
    ).wait_send()


def shards(contributions, routes, slots, panels):
    rows, width = contributions.shape
    nodes = panels.shape[0]
    devices = lax.axis_size("fluid") * lax.axis_size("patch")
    bf16, f32, i32 = jnp.bfloat16, jnp.float32, jnp.int32
    strip = width // PLANE
    vmem = pl.BlockSpec(memory_space=pltpu.VMEM)
    dma = pltpu.SemaphoreType.DMA
    return pl.pallas_call(
        functools.partial(kernel, 0.5 / math.sqrt(nodes * devices)),
        out_shape=(
            jax.ShapeDtypeStruct((nodes, width), bf16),
            jax.ShapeDtypeStruct((width, width), f32),
        ),
        in_specs=[vmem, vmem, vmem, pl.BlockSpec(memory_space=pl.ANY)],
        out_specs=(vmem, vmem),
        scratch_shapes=[
            pltpu.VMEM((2 * rows, width), bf16),
            pltpu.VMEM((2 * rows, width), bf16),
            pltpu.VMEM((128, rows), bf16),
            pltpu.VMEM((1, rows), i32),
            pltpu.VMEM((128, 128), i32),
            pltpu.VMEM((COLUMN, PLANE, 128), i32),
            pltpu.VMEM((PLANE, 8, 128), i32),
            pltpu.VMEM((PLANE, 8, 128), i32),
            pltpu.VMEM((nodes, width), f32),
            pltpu.VMEM((PLANE, nodes, width), bf16),
            pltpu.VMEM((PLANE, nodes, nodes), bf16),
            pltpu.VMEM((nodes, width), f32),
            pltpu.VMEM((width, width), f32),
            pltpu.VMEM((PLANE, strip, width), f32),
            pltpu.VMEM((COLUMN, strip, width), f32),
            pltpu.VMEM((width, width), f32),
            dma, dma((PLANE,)), dma((COLUMN,)), dma((COLUMN,)), dma((PLANE,)), dma((PLANE,)),
            dma, dma((PLANE * 4,)), dma((PLANE,)),
            dma((PLANE,)), dma((PLANE,)), dma((COLUMN,)), dma((COLUMN,)), dma((PLANE,)), dma((PLANE,)),
        ],
        compiler_params=pltpu.CompilerParams(
            collective_id=0, has_side_effects=True, vmem_limit_bytes=60 * 1024 * 1024
        ),
        cost_estimate=pl.CostEstimate(
            flops=2 * nodes * PLANE * nodes * width, bytes_accessed=nodes * nodes * PLANE * 2, transcendentals=0
        ),
    )(contributions, routes.reshape(1, rows), slots.reshape(1, rows), panels)


def solution(mesh):
    placed = (
        P(("fluid", "patch"), None),
        P(("fluid", "patch"), None),
        P(("fluid", "patch")),
        P(("fluid", "patch"), None),
    )
    return jax.shard_map(
        shards,
        mesh=mesh,
        in_specs=placed,
        out_specs=(P(("fluid", "patch"), None), P()),
        check_vma=False,
    )
```

```python
import functools
import math

import jax
import jax.numpy as jnp
from jax import lax
from jax.experimental import pallas as pl
from jax.experimental.pallas import tpu as pltpu
from jax.sharding import PartitionSpec as P

MESH = pl.DeviceIdType.MESH
SIDE = 4
COLUMN = 8
PLANE = 16
CAP = 32
STRIDE = 5


def where_am_i():
    f, p = lax.axis_index("fluid"), lax.axis_index("patch")
    return f // 2, lax.rem(f, 2), p // SIDE, lax.rem(p, SIDE)


def shifted(column_step, plane_step, sign=1):
    z, c, x, y = where_am_i()
    dz, dc = column_step // 2, column_step % 2
    dx, dy = plane_step // SIDE, plane_step % SIDE
    if sign < 0:
        dz, dx, dy = SIDE - dz, SIDE - dx, SIDE - dy
    return (
        lax.rem(z + dz, SIDE) * 2 + lax.rem(c + dc, 2),
        lax.rem(x + dx, SIDE) * SIDE + lax.rem(y + dy, SIDE),
    )


def kernel(
    contributions, routes, slots, panels, traces, mass,
    out_rows, in_rows, onehot, position, slot_out, column_slots, plane_out, plane_slots, landed,
    gathered, panel_v, coupled, own_t, share, other, reduce_in, column_in, full, entered,
    row_send, row_recv, slot_send, slot_recv, plane_send, plane_recv, gather_send, gather_recv, panel_sem,
    core_send, core_recv, reduce_send, reduce_recv, column_send, column_recv, full_send, full_recv,
):
    f32, bf16, i32 = jnp.float32, jnp.bfloat16, jnp.int32
    f, p = lax.axis_index("fluid"), lax.axis_index("patch")
    z, c, x, y = where_am_i()
    rows = contributions.shape[0]
    nodes = traces.shape[0]
    width = traces.shape[1]
    half, piece = nodes // 2, nodes // 4

    barrier = pltpu.get_barrier_semaphore()

    for s in range(1, PLANE):
        pl.semaphore_signal(barrier, inc=1, device_id=shifted(0, s), device_id_type=MESH)
    for w in range(1, COLUMN):
        pl.semaphore_signal(barrier, inc=1, device_id=shifted(w, 0), device_id_type=MESH)

    panel_copies = []
    for s in range(PLANE):
        dx, dy = s // SIDE, s % SIDE
        owner = lax.rem(x + SIDE - dx, SIDE) * SIDE + lax.rem(y + SIDE - dy, SIDE)
        copy = pltpu.make_async_copy(
            panels.at[:, pl.ds(pl.multiple_of(owner * nodes, 128), nodes)], panel_v.at[s], panel_sem.at[s]
        )
        copy.start()
        panel_copies.append(copy)

    to = routes[...]
    to_f, to_p = to >> 4, to & 15
    dz, dc = ((to_f >> 1) - z) & 3, ((to_f & 1) - c) & 1
    dx, dy = ((to_p >> 2) - x) & 3, ((to_p & 3) - y) & 3
    step_column, step_plane = dz * 2 + dc, dx * 4 + dy
    label = step_column * PLANE + step_plane
    onehot[...] = (lax.broadcasted_iota(i32, (128, rows), 0) == label).astype(bf16)
    block = 256
    pl.semaphore_wait(barrier, PLANE + COLUMN - 2)
    for w in range(1, COLUMN):
        pl.semaphore_signal(entered, inc=1, device_id=shifted(w, 0), device_id_type=MESH)

    upper = (
        lax.broadcasted_iota(i32, (block, block), 0) < lax.broadcasted_iota(i32, (block, block), 1)
    ).astype(bf16)
    seen = jnp.zeros((128, 1), f32)
    orders = []
    for b in range(rows // block):
        mine = onehot[:, b * block:(b + 1) * block]
        before = jnp.dot(mine, upper, preferred_element_type=f32) + seen
        wide = mine.astype(f32)
        orders.append(jnp.sum(wide * before, axis=0, keepdims=True))
        seen = seen + jnp.sum(wide, axis=1, keepdims=True)
    order = jnp.concatenate(orders, axis=1).astype(i32)
    turn = (step_plane - STRIDE * step_column) & 15
    position[...] = (turn * COLUMN + step_column) * CAP + order

    pl.semaphore_wait(entered, COLUMN - 1)

    def build(kk):
        i = lax.broadcasted_iota(i32, (256, 1), 0)
        pick = (kk * 256 + i == position[...]).astype(bf16)
        made = jnp.dot(pick, contributions[...], preferred_element_type=f32).astype(bf16)
        out_rows[pl.ds(pl.multiple_of(kk * 256, 256), 256), :] = made

    def row_copy(kk, w):
        at = pl.ds(pl.multiple_of(kk * 256 + w * CAP, CAP), CAP)
        return pltpu.make_async_remote_copy(
            src_ref=out_rows.at[at], dst_ref=in_rows.at[at],
            send_sem=row_send, recv_sem=row_recv.at[kk],
            device_id=shifted(w, lax.rem(kk + STRIDE * w, PLANE)), device_id_type=MESH,
        )

    def send_rows(first, last):
        @pl.loop(first, last)
        def _(kk):
            build(kk)
            for w in range(COLUMN):
                row_copy(kk, w).start()

    send_rows(1, 3)

    value = slots[...] + 1
    lane_order = lax.broadcasted_iota(i32, (128, rows), 0) & (CAP - 1)
    hit = lane_order == order
    nt = (((1,), (1,)), ((), ()))
    high = jnp.where(hit, (value >> 5).astype(f32), 0.0).astype(bf16)
    table = lax.dot_general(onehot[...], high, nt, preferred_element_type=f32) * 32.0
    low = jnp.where(hit, (value & 31).astype(f32), 0.0).astype(bf16)
    table = table + lax.dot_general(onehot[...], low, nt, preferred_element_type=f32)
    lane_group = lax.broadcasted_iota(i32, (128, 128), 1) >> 5
    row_group = (lax.broadcasted_iota(i32, (128, 128), 0) >> 4) & 3
    slot_out[...] = jnp.where(lane_group == row_group, table, 0.0).astype(i32)
    column_slots[0] = slot_out[0:PLANE]

    slot_copies = []
    for w in range(1, COLUMN):
        copy = pltpu.make_async_remote_copy(
            src_ref=slot_out.at[pl.ds(w * PLANE, PLANE)], dst_ref=column_slots.at[w],
            send_sem=slot_send.at[w], recv_sem=slot_recv.at[w], device_id=shifted(w, 0), device_id_type=MESH,
        )
        copy.start()
        slot_copies.append(copy)

    send_rows(3, 9)

    for copy in slot_copies:
        copy.wait()
    first = column_slots[0] + column_slots[1] + column_slots[2] + column_slots[3]
    second = column_slots[4] + column_slots[5] + column_slots[6] + column_slots[7]
    sub = lax.broadcasted_iota(i32, (PLANE, 8, 128), 1)
    plane_out[...] = jnp.where(sub < 4, first[:, None, :], second[:, None, :])
    plane_slots[0] = plane_out[0]
    plane_copies = []
    for s in range(1, PLANE):
        copy = pltpu.make_async_remote_copy(
            src_ref=plane_out.at[s], dst_ref=plane_slots.at[s],
            send_sem=plane_send.at[s], recv_sem=plane_recv.at[s], device_id=shifted(0, s), device_id_type=MESH,
        )
        copy.start()
        plane_copies.append(copy)

    send_rows(9, PLANE)
    build(0)
    for w in range(1, COLUMN):
        row_copy(0, w).start()
    in_rows[0:CAP, :] = out_rows[0:CAP, :]

    for copy in plane_copies:
        copy.wait()

    landed[...] = jnp.zeros_like(landed)

    def land(kk):
        group = lax.broadcasted_iota(i32, (1, 128), 1) >> 5
        parts = []
        for side in range(2):
            row = jnp.zeros((1, 128), i32)
            for k in range(4):
                w = side * 4 + k
                got = plane_slots[lax.rem(kk + STRIDE * w, PLANE), pl.ds(side * 4, 1), :]
                row = row + jnp.where(group == k, got, 0)
            parts.append(row)
        names = jnp.concatenate(parts, axis=1) - 1
        spread = (lax.broadcasted_iota(i32, (nodes, 256), 0) == names).astype(bf16)
        landed[...] += jnp.dot(
            spread, in_rows[pl.ds(pl.multiple_of(kk * 256, 256), 256), :], preferred_element_type=f32
        )

    def arrival(kk, start, count):
        at = pl.ds(start, count)
        return pltpu.make_async_remote_copy(
            src_ref=in_rows.at[at], dst_ref=in_rows.at[at],
            send_sem=row_send, recv_sem=row_recv.at[kk], device_id=(f, p), device_id_type=MESH,
        )

    @pl.loop(1, PLANE)
    def _(kk):
        arrival(kk, pl.multiple_of(kk * 256, 256), 256).wait_recv()
        land(kk)

    arrival(0, CAP, 256 - CAP).wait_recv()
    land(0)
    own = landed[...].astype(bf16)
    gathered[0] = own

    sent = []

    def pass_on(axis, direction, source, start, count, sem):
        dx, dy = source
        if axis == 0:
            dx = (dx + direction) % SIDE
            device = (f, lax.rem(x + direction + SIDE, SIDE) * SIDE + y)
        else:
            dy = (dy + direction) % SIDE
            device = (f, x * SIDE + lax.rem(y + direction + SIDE, SIDE))
        at = pl.ds(start, count)
        copy = pltpu.make_async_remote_copy(
            src_ref=gathered.at[source[0] * SIDE + source[1], at], dst_ref=gathered.at[dx * SIDE + dy, at],
            send_sem=gather_send, recv_sem=gather_recv.at[(dx * SIDE + dy) * 4 + sem],
            device_id=device, device_id_type=MESH,
        )
        copy.start()
        sent.append(count)

    def await_piece(source, start, count, sem):
        s = source[0] * SIDE + source[1]
        at = pl.ds(start, count)
        pltpu.make_async_remote_copy(
            src_ref=gathered.at[s, at], dst_ref=gathered.at[s, at],
            send_sem=gather_send, recv_sem=gather_recv.at[s * 4 + sem], device_id=(f, p), device_id_type=MESH,
        ).wait_recv()

    def at(lead, a, b):
        return (a, b) if lead == 0 else (b, a)

    def send_half(lead, axis, direction, source):
        pass_on(axis, direction, source, lead * half, half, lead * 2)

    def send_piece(lead, axis, direction, source, k):
        pass_on(axis, direction, source, lead * half + k * piece, piece, lead * 2 + k)

    def wait_half(lead, source):
        await_piece(source, lead * half, half, lead * 2)

    def wait_piece(lead, source, k):
        await_piece(source, lead * half + k * piece, piece, lead * 2 + k)

    def multiply(s, start, count):
        coupled[...] += jnp.dot(
            panel_v[s, :, pl.ds(start, count)], gathered[s, pl.ds(start, count), :], preferred_element_type=f32
        )

    for lead in (0, 1):
        for direction in (1, -1):
            send_half(lead, lead, direction, (0, 0))
            send_half(lead, 1 - lead, direction, (0, 0))
    traces[...] = own
    own_t[...] = own.T
    coupled[...] = jnp.zeros_like(coupled)
    for copy in panel_copies:
        copy.wait()
    multiply(0, 0, nodes)

    def multiply_halves(places):
        for lead, place in places:
            multiply(place[0] * SIDE + place[1], lead * half, half)

    for k, a, direction in ((0, 1, 1), (1, 3, -1)):
        for lead in (0, 1):
            place = at(lead, a, 0)
            wait_half(lead, place)
            send_piece(lead, lead, direction, place, k)
            send_half(lead, 1 - lead, 1, place)
            send_half(lead, 1 - lead, -1, place)
    for k, b, direction in ((0, 1, 1), (1, 3, -1)):
        for lead in (0, 1):
            place = at(lead, 0, b)
            wait_half(lead, place)
            send_piece(lead, 1 - lead, direction, place, k)
    multiply_halves([(lead, at(lead, a, b)) for a, b in ((1, 0), (3, 0), (0, 1), (0, 3)) for lead in (0, 1)])
    for k in (0, 1):
        for lead in (0, 1):
            place = at(lead, 2, 0)
            wait_piece(lead, place, k)
            send_piece(lead, 1 - lead, 1, place, k)
            send_piece(lead, 1 - lead, -1, place, k)
    multiply_halves([(lead, at(lead, 2, 0)) for lead in (0, 1)])
    for a in (1, 3):
        for k, b, direction in ((0, 1, 1), (1, 3, -1)):
            for lead in (0, 1):
                place = at(lead, a, b)
                wait_half(lead, place)
                send_piece(lead, 1 - lead, direction, place, k)
        multiply_halves([(lead, at(lead, a, b)) for b in (1, 3) for lead in (0, 1)])
    for k in (0, 1):
        for lead in (0, 1):
            wait_piece(lead, at(lead, 0, 2), k)
    multiply_halves([(lead, at(lead, 0, 2)) for lead in (0, 1)])
    for lead in (0, 1):
        place = at(lead, 2, 1)
        wait_piece(lead, place, 0)
        send_piece(lead, 1 - lead, 1, place, 0)
        place = at(lead, 2, 3)
        wait_piece(lead, place, 1)
        send_piece(lead, 1 - lead, -1, place, 1)
    for lead in (0, 1):
        wait_piece(lead, at(lead, 2, 1), 1)
        wait_piece(lead, at(lead, 2, 3), 0)
    multiply_halves([(lead, at(lead, 2, b)) for b in (1, 3) for lead in (0, 1)])
    for a in (1, 3):
        for k in (0, 1):
            for lead in (0, 1):
                wait_piece(lead, at(lead, a, 2), k)
        multiply_halves([(lead, at(lead, a, 2)) for lead in (0, 1)])
    for k in (0, 1):
        for lead in (0, 1):
            wait_piece(lead, at(lead, 2, 2), k)
    multiply_halves([(lead, at(lead, 2, 2)) for lead in (0, 1)])

    top = coupled[...].astype(bf16)
    rest = (coupled[...] - top.astype(f32)).astype(bf16)
    side = width // 2

    def share_of(core):
        left = own_t[pl.ds(pl.multiple_of(core * side, side), side), :]
        return jnp.dot(left, top, preferred_element_type=f32) + jnp.dot(left, rest, preferred_element_type=f32)

    share[...] = share_of(1 - c)
    copy = pltpu.make_async_remote_copy(
        src_ref=share, dst_ref=other, send_sem=core_send.at[0], recv_sem=core_recv.at[0],
        device_id=shifted(1, 0), device_id_type=MESH,
    )
    copy.start()
    half_share = share_of(c)
    copy.wait()
    share[...] = half_share + other[...]

    strip = side // PLANE
    copies = []
    for s in range(1, PLANE):
        device = shifted(0, s)
        copy = pltpu.make_async_remote_copy(
            src_ref=share.at[pl.ds(pl.multiple_of(device[1] * strip, strip), strip)], dst_ref=reduce_in.at[s],
            send_sem=reduce_send.at[s], recv_sem=reduce_recv.at[s], device_id=device, device_id_type=MESH,
        )
        copy.start()
        copies.append(copy)
    total = share[pl.ds(pl.multiple_of(p * strip, strip), strip), :]
    for s, copy in enumerate(copies):
        copy.wait()
        total = total + reduce_in[s + 1]
    column_in[z] = total
    copies = []
    for step in range(1, SIDE):
        copy = pltpu.make_async_remote_copy(
            src_ref=column_in.at[z], dst_ref=column_in.at[z],
            send_sem=column_send.at[step], recv_sem=column_recv.at[step],
            device_id=shifted(2 * step, 0), device_id_type=MESH,
        )
        copy.start()
        copies.append(copy)
    for copy in copies:
        copy.wait()
    total = column_in[0]
    for step in range(1, SIDE):
        total = total + column_in[step]
    mine = pl.ds(pl.multiple_of(c * side + p * strip, strip), strip)
    full[mine, :] = total
    copies = []
    for s in range(1, PLANE):
        copy = pltpu.make_async_remote_copy(
            src_ref=full.at[mine], dst_ref=full.at[mine],
            send_sem=full_send.at[s], recv_sem=full_recv.at[s], device_id=shifted(0, s), device_id_type=MESH,
        )
        copy.start()
        copies.append(copy)
    for copy in copies:
        copy.wait()
    mine = pl.ds(pl.multiple_of(c * side, side), side)
    copy = pltpu.make_async_remote_copy(
        src_ref=full.at[mine], dst_ref=full.at[mine], send_sem=core_send.at[1], recv_sem=core_recv.at[1],
        device_id=shifted(1, 0), device_id_type=MESH,
    )
    copy.start()
    copy.wait()
    mass[...] = full[...]

    everything = pl.ds(CAP, rows * 2 - CAP)
    pltpu.make_async_remote_copy(
        src_ref=out_rows.at[everything], dst_ref=out_rows.at[everything],
        send_sem=row_send, recv_sem=row_recv.at[0], device_id=(f, p), device_id_type=MESH,
    ).wait_send()
    assert sum(sent) % nodes == 0
    blocks = pl.ds(0, sum(sent) // nodes)
    pltpu.make_async_remote_copy(
        src_ref=gathered.at[blocks], dst_ref=gathered.at[blocks],
        send_sem=gather_send, recv_sem=gather_recv.at[0], device_id=(f, p), device_id_type=MESH,
    ).wait_send()


def finish(factor, traces, summed, traces_out, mass):
    traces_out[...] = traces[...]
    mass[...] = (summed[...] + summed[...].T) * factor


def shards(contributions, routes, slots, panels):
    rows, width = contributions.shape
    nodes = panels.shape[0]
    devices = lax.axis_size("fluid") * lax.axis_size("patch")
    bf16, f32, i32 = jnp.bfloat16, jnp.float32, jnp.int32
    strip = width // 2 // PLANE
    vmem = pl.BlockSpec(memory_space=pltpu.VMEM)
    dma = pltpu.SemaphoreType.DMA
    summed = pl.pallas_call(
        kernel,
        out_shape=(
            jax.ShapeDtypeStruct((nodes, width), bf16),
            jax.ShapeDtypeStruct((width, width), f32),
        ),
        in_specs=[vmem, vmem, vmem, pl.BlockSpec(memory_space=pl.ANY)],
        out_specs=(vmem, vmem),
        scratch_shapes=[
            pltpu.VMEM((2 * rows, width), bf16),
            pltpu.VMEM((2 * rows, width), bf16),
            pltpu.VMEM((128, rows), bf16),
            pltpu.VMEM((1, rows), i32),
            pltpu.VMEM((128, 128), i32),
            pltpu.VMEM((COLUMN, PLANE, 128), i32),
            pltpu.VMEM((PLANE, 8, 128), i32),
            pltpu.VMEM((PLANE, 8, 128), i32),
            pltpu.VMEM((nodes, width), f32),
            pltpu.VMEM((PLANE, nodes, width), bf16),
            pltpu.VMEM((PLANE, nodes, nodes), bf16),
            pltpu.VMEM((nodes, width), f32),
            pltpu.VMEM((width, nodes), bf16),
            pltpu.VMEM((width // 2, width), f32),
            pltpu.VMEM((width // 2, width), f32),
            pltpu.VMEM((PLANE, strip, width), f32),
            pltpu.VMEM((SIDE, strip, width), f32),
            pltpu.VMEM((width, width), f32),
            pltpu.SemaphoreType.REGULAR,
            dma, dma((PLANE,)), dma((COLUMN,)), dma((COLUMN,)), dma((PLANE,)), dma((PLANE,)),
            dma, dma((PLANE * 4,)), dma((PLANE,)),
            dma((2,)), dma((2,)), dma((PLANE,)), dma((PLANE,)), dma((SIDE,)), dma((SIDE,)), dma((PLANE,)), dma((PLANE,)),
        ],
        compiler_params=pltpu.CompilerParams(
            collective_id=0, has_side_effects=True, vmem_limit_bytes=60 * 1024 * 1024
        ),
        cost_estimate=pl.CostEstimate(
            flops=2 * nodes * PLANE * nodes * width, bytes_accessed=nodes * nodes * PLANE * 2, transcendentals=0
        ),
    )(contributions, routes.reshape(1, rows), slots.reshape(1, rows), panels)
    return pl.pallas_call(
        functools.partial(finish, 0.5 / math.sqrt(nodes * devices)),
        out_shape=(
            jax.ShapeDtypeStruct((nodes, width), bf16),
            jax.ShapeDtypeStruct((width, width), f32),
        ),
        in_specs=[vmem, vmem],
        out_specs=(vmem, vmem),
    )(*summed)


def solution(mesh):
    placed = (
        P(("fluid", "patch"), None),
        P(("fluid", "patch"), None),
        P(("fluid", "patch")),
        P(("fluid", "patch"), None),
    )
    return jax.shard_map(
        shards,
        mesh=mesh,
        in_specs=placed,
        out_specs=(P(("fluid", "patch"), None), P()),
        check_vma=False,
    )
```

```python
import functools
import math

import jax
import jax.numpy as jnp
from jax import lax
from jax.experimental import pallas as pl
from jax.experimental.pallas import tpu as pltpu
from jax.sharding import PartitionSpec as P

MESH = pl.DeviceIdType.MESH
SIDE = 4
COLUMN = 8
PLANE = 16
CAP = 32
STRIDE = 5


def where_am_i():
    f, p = lax.axis_index("fluid"), lax.axis_index("patch")
    return f // 2, lax.rem(f, 2), p // SIDE, lax.rem(p, SIDE)


def shifted(column_step, plane_step, sign=1):
    z, c, x, y = where_am_i()
    dz, dc = column_step // 2, column_step % 2
    dx, dy = plane_step // SIDE, plane_step % SIDE
    if sign < 0:
        dz, dx, dy = SIDE - dz, SIDE - dx, SIDE - dy
    return (
        lax.rem(z + dz, SIDE) * 2 + lax.rem(c + dc, 2),
        lax.rem(x + dx, SIDE) * SIDE + lax.rem(y + dy, SIDE),
    )


def kernel(
    contributions_in, routes, slots, panels, traces, mass,
    contributions, out_rows, in_rows, onehot, position, slot_out, column_slots, plane_out, plane_slots, landed,
    gathered, panel_v, coupled, own_t, share, share_sent, reduce_in, column_in, full, entered,
    row_send, row_recv, slot_send, slot_recv, plane_send, plane_recv, gather_send, gather_recv, panel_sem,
    local_sem, reduce_send, reduce_recv, column_send, column_recv, full_send, full_recv,
):
    f32, bf16, i32 = jnp.float32, jnp.bfloat16, jnp.int32
    f, p = lax.axis_index("fluid"), lax.axis_index("patch")
    z, c, x, y = where_am_i()
    rows = contributions_in.shape[0]
    nodes = traces.shape[0]
    width = traces.shape[1]
    half, piece = nodes // 2, nodes // 4

    barrier = pltpu.get_barrier_semaphore()

    for s in range(1, PLANE):
        pl.semaphore_signal(barrier, inc=1, device_id=shifted(0, s), device_id_type=MESH)
    for w in range(1, COLUMN):
        pl.semaphore_signal(barrier, inc=1, device_id=shifted(w, 0), device_id_type=MESH)

    rows_copy = pltpu.make_async_copy(contributions_in, contributions, local_sem.at[0])
    rows_copy.start()

    panel_copies = []
    for s in range(PLANE):
        dx, dy = s // SIDE, s % SIDE
        owner = lax.rem(x + SIDE - dx, SIDE) * SIDE + lax.rem(y + SIDE - dy, SIDE)
        copy = pltpu.make_async_copy(
            panels.at[:, pl.ds(pl.multiple_of(owner * nodes, 128), nodes)], panel_v.at[s], panel_sem.at[s]
        )
        copy.start()
        panel_copies.append(copy)

    to = routes[...]
    to_f, to_p = to >> 4, to & 15
    dz, dc = ((to_f >> 1) - z) & 3, ((to_f & 1) - c) & 1
    dx, dy = ((to_p >> 2) - x) & 3, ((to_p & 3) - y) & 3
    step_column, step_plane = dz * 2 + dc, dx * 4 + dy
    label = step_column * PLANE + step_plane
    onehot[...] = (lax.broadcasted_iota(i32, (128, rows), 0) == label).astype(bf16)
    block = 256
    pl.semaphore_wait(barrier, PLANE + COLUMN - 2)
    for w in range(1, COLUMN):
        pl.semaphore_signal(entered, inc=1, device_id=shifted(w, 0), device_id_type=MESH)

    upper = (
        lax.broadcasted_iota(i32, (block, block), 0) < lax.broadcasted_iota(i32, (block, block), 1)
    ).astype(bf16)
    seen = jnp.zeros((128, 1), f32)
    orders = []
    for b in range(rows // block):
        mine = onehot[:, b * block:(b + 1) * block]
        before = jnp.dot(mine, upper, preferred_element_type=f32) + seen
        wide = mine.astype(f32)
        orders.append(jnp.sum(wide * before, axis=0, keepdims=True))
        seen = seen + jnp.sum(wide, axis=1, keepdims=True)
    order = jnp.concatenate(orders, axis=1).astype(i32)
    turn = (step_plane - STRIDE * step_column) & 15
    position[...] = (turn * COLUMN + step_column) * CAP + order

    rows_copy.wait()
    pl.semaphore_wait(entered, COLUMN - 1)

    def build(kk):
        i = lax.broadcasted_iota(i32, (256, 1), 0)
        pick = (kk * 256 + i == position[...]).astype(bf16)
        made = jnp.dot(pick, contributions[...], preferred_element_type=f32).astype(bf16)
        out_rows[pl.ds(pl.multiple_of(kk * 256, 256), 256), :] = made

    def row_copy(kk, w):
        at = pl.ds(pl.multiple_of(kk * 256 + w * CAP, CAP), CAP)
        return pltpu.make_async_remote_copy(
            src_ref=out_rows.at[at], dst_ref=in_rows.at[at],
            send_sem=row_send, recv_sem=row_recv.at[kk],
            device_id=shifted(w, lax.rem(kk + STRIDE * w, PLANE)), device_id_type=MESH,
        )

    def send_rows(first, last):
        @pl.loop(first, last)
        def _(kk):
            build(kk)
            for w in range(COLUMN):
                row_copy(kk, w).start()

    send_rows(1, 3)

    value = slots[...] + 1
    lane_order = lax.broadcasted_iota(i32, (128, rows), 0) & (CAP - 1)
    hit = lane_order == order
    nt = (((1,), (1,)), ((), ()))
    high = jnp.where(hit, (value >> 5).astype(f32), 0.0).astype(bf16)
    table = lax.dot_general(onehot[...], high, nt, preferred_element_type=f32) * 32.0
    low = jnp.where(hit, (value & 31).astype(f32), 0.0).astype(bf16)
    table = table + lax.dot_general(onehot[...], low, nt, preferred_element_type=f32)
    lane_group = lax.broadcasted_iota(i32, (128, 128), 1) >> 5
    row_group = (lax.broadcasted_iota(i32, (128, 128), 0) >> 4) & 3
    slot_out[...] = jnp.where(lane_group == row_group, table, 0.0).astype(i32)
    column_slots[0] = slot_out[0:PLANE]

    slot_copies = []
    for w in range(1, COLUMN):
        copy = pltpu.make_async_remote_copy(
            src_ref=slot_out.at[pl.ds(w * PLANE, PLANE)], dst_ref=column_slots.at[w],
            send_sem=slot_send.at[w], recv_sem=slot_recv.at[w], device_id=shifted(w, 0), device_id_type=MESH,
        )
        copy.start()
        slot_copies.append(copy)

    send_rows(3, 9)

    for copy in slot_copies:
        copy.wait()
    first = column_slots[0] + column_slots[1] + column_slots[2] + column_slots[3]
    second = column_slots[4] + column_slots[5] + column_slots[6] + column_slots[7]
    sub = lax.broadcasted_iota(i32, (PLANE, 8, 128), 1)
    plane_out[...] = jnp.where(sub < 4, first[:, None, :], second[:, None, :])
    plane_slots[0] = plane_out[0]
    plane_copies = []
    for s in range(1, PLANE):
        copy = pltpu.make_async_remote_copy(
            src_ref=plane_out.at[s], dst_ref=plane_slots.at[s],
            send_sem=plane_send.at[s], recv_sem=plane_recv.at[s], device_id=shifted(0, s), device_id_type=MESH,
        )
        copy.start()
        plane_copies.append(copy)

    send_rows(9, PLANE)
    build(0)
    for w in range(1, COLUMN):
        row_copy(0, w).start()
    in_rows[0:CAP, :] = out_rows[0:CAP, :]

    for copy in plane_copies:
        copy.wait()

    landed[...] = jnp.zeros_like(landed)

    def land(kk):
        group = lax.broadcasted_iota(i32, (1, 128), 1) >> 5
        parts = []
        for side in range(2):
            row = jnp.zeros((1, 128), i32)
            for k in range(4):
                w = side * 4 + k
                got = plane_slots[lax.rem(kk + STRIDE * w, PLANE), pl.ds(side * 4, 1), :]
                row = row + jnp.where(group == k, got, 0)
            parts.append(row)
        names = jnp.concatenate(parts, axis=1) - 1
        spread = (lax.broadcasted_iota(i32, (nodes, 256), 0) == names).astype(bf16)
        landed[...] += jnp.dot(
            spread, in_rows[pl.ds(pl.multiple_of(kk * 256, 256), 256), :], preferred_element_type=f32
        )

    def arrival(kk, start, count):
        at = pl.ds(start, count)
        return pltpu.make_async_remote_copy(
            src_ref=in_rows.at[at], dst_ref=in_rows.at[at],
            send_sem=row_send, recv_sem=row_recv.at[kk], device_id=(f, p), device_id_type=MESH,
        )

    @pl.loop(1, PLANE)
    def _(kk):
        arrival(kk, pl.multiple_of(kk * 256, 256), 256).wait_recv()
        land(kk)

    arrival(0, CAP, 256 - CAP).wait_recv()
    land(0)
    own = landed[...].astype(bf16)
    gathered[0] = own

    sent = []

    def pass_on(axis, direction, source, start, count, sem):
        dx, dy = source
        if axis == 0:
            dx = (dx + direction) % SIDE
            device = (f, lax.rem(x + direction + SIDE, SIDE) * SIDE + y)
        else:
            dy = (dy + direction) % SIDE
            device = (f, x * SIDE + lax.rem(y + direction + SIDE, SIDE))
        at = pl.ds(start, count)
        copy = pltpu.make_async_remote_copy(
            src_ref=gathered.at[source[0] * SIDE + source[1], at], dst_ref=gathered.at[dx * SIDE + dy, at],
            send_sem=gather_send, recv_sem=gather_recv.at[(dx * SIDE + dy) * 4 + sem],
            device_id=device, device_id_type=MESH,
        )
        copy.start()
        sent.append(count)

    def await_piece(source, start, count, sem):
        s = source[0] * SIDE + source[1]
        at = pl.ds(start, count)
        pltpu.make_async_remote_copy(
            src_ref=gathered.at[s, at], dst_ref=gathered.at[s, at],
            send_sem=gather_send, recv_sem=gather_recv.at[s * 4 + sem], device_id=(f, p), device_id_type=MESH,
        ).wait_recv()

    def at(lead, a, b):
        return (a, b) if lead == 0 else (b, a)

    def send_half(lead, axis, direction, source):
        pass_on(axis, direction, source, lead * half, half, lead * 2)

    def send_piece(lead, axis, direction, source, k):
        pass_on(axis, direction, source, lead * half + k * piece, piece, lead * 2 + k)

    def wait_half(lead, source):
        await_piece(source, lead * half, half, lead * 2)

    def wait_piece(lead, source, k):
        await_piece(source, lead * half + k * piece, piece, lead * 2 + k)

    def multiply(s, start, count):
        coupled[...] += jnp.dot(
            panel_v[s, :, pl.ds(start, count)], gathered[s, pl.ds(start, count), :], preferred_element_type=f32
        )

    for lead in (0, 1):
        for direction in (1, -1):
            send_half(lead, lead, direction, (0, 0))
            send_half(lead, 1 - lead, direction, (0, 0))
    traces_copy = pltpu.make_async_copy(gathered.at[0], traces, local_sem.at[1])
    traces_copy.start()
    own_t[...] = own.T
    coupled[...] = jnp.zeros_like(coupled)
    for copy in panel_copies:
        copy.wait()
    multiply(0, 0, nodes)

    def multiply_halves(places):
        for lead, place in places:
            multiply(place[0] * SIDE + place[1], lead * half, half)

    for k, a, direction in ((0, 1, 1), (1, 3, -1)):
        for lead in (0, 1):
            place = at(lead, a, 0)
            wait_half(lead, place)
            send_piece(lead, lead, direction, place, k)
            send_half(lead, 1 - lead, 1, place)
            send_half(lead, 1 - lead, -1, place)
    for k, b, direction in ((0, 1, 1), (1, 3, -1)):
        for lead in (0, 1):
            place = at(lead, 0, b)
            wait_half(lead, place)
            send_piece(lead, 1 - lead, direction, place, k)
    multiply_halves([(lead, at(lead, a, b)) for a, b in ((1, 0), (3, 0), (0, 1), (0, 3)) for lead in (0, 1)])
    for k in (0, 1):
        for lead in (0, 1):
            place = at(lead, 2, 0)
            wait_piece(lead, place, k)
            send_piece(lead, 1 - lead, 1, place, k)
            send_piece(lead, 1 - lead, -1, place, k)
    multiply_halves([(lead, at(lead, 2, 0)) for lead in (0, 1)])
    for a in (1, 3):
        for k, b, direction in ((0, 1, 1), (1, 3, -1)):
            for lead in (0, 1):
                place = at(lead, a, b)
                wait_half(lead, place)
                send_piece(lead, 1 - lead, direction, place, k)
        multiply_halves([(lead, at(lead, a, b)) for b in (1, 3) for lead in (0, 1)])
    for k in (0, 1):
        for lead in (0, 1):
            wait_piece(lead, at(lead, 0, 2), k)
    multiply_halves([(lead, at(lead, 0, 2)) for lead in (0, 1)])
    for lead in (0, 1):
        place = at(lead, 2, 1)
        wait_piece(lead, place, 0)
        send_piece(lead, 1 - lead, 1, place, 0)
        place = at(lead, 2, 3)
        wait_piece(lead, place, 1)
        send_piece(lead, 1 - lead, -1, place, 1)
    for lead in (0, 1):
        wait_piece(lead, at(lead, 2, 1), 1)
        wait_piece(lead, at(lead, 2, 3), 0)
    multiply_halves([(lead, at(lead, 2, b)) for b in (1, 3) for lead in (0, 1)])
    for a in (1, 3):
        for k in (0, 1):
            for lead in (0, 1):
                wait_piece(lead, at(lead, a, 2), k)
        multiply_halves([(lead, at(lead, a, 2)) for lead in (0, 1)])
    for k in (0, 1):
        for lead in (0, 1):
            wait_piece(lead, at(lead, 2, 2), k)
    multiply_halves([(lead, at(lead, 2, 2)) for lead in (0, 1)])

    top = coupled[...].astype(bf16)
    rest = (coupled[...] - top.astype(f32)).astype(bf16)
    share[...] = jnp.dot(own_t[...], top, preferred_element_type=f32) + jnp.dot(
        own_t[...], rest, preferred_element_type=f32
    )
    share_sent[...] = share[...].astype(bf16)

    strip = width // PLANE
    copies = []
    for s in range(1, PLANE):
        device = shifted(0, s)
        copy = pltpu.make_async_remote_copy(
            src_ref=share_sent.at[pl.ds(pl.multiple_of(device[1] * strip, strip), strip)], dst_ref=reduce_in.at[s],
            send_sem=reduce_send.at[s], recv_sem=reduce_recv.at[s], device_id=device, device_id_type=MESH,
        )
        copy.start()
        copies.append(copy)
    mine = pl.ds(pl.multiple_of(p * strip, strip), strip)
    total = share[mine, :]
    for s, copy in enumerate(copies):
        copy.wait()
        total = total + reduce_in[s + 1].astype(f32)
    column_in[f] = total.astype(bf16)
    copies = []
    for w in range(1, COLUMN):
        copy = pltpu.make_async_remote_copy(
            src_ref=column_in.at[f], dst_ref=column_in.at[f],
            send_sem=column_send.at[w], recv_sem=column_recv.at[w], device_id=shifted(w, 0), device_id_type=MESH,
        )
        copy.start()
        copies.append(copy)
    for copy in copies:
        copy.wait()
    total = column_in[0].astype(f32)
    for w in range(1, COLUMN):
        total = total + column_in[w].astype(f32)
    full[mine, :] = total.astype(bf16)
    copies = []
    for s in range(1, PLANE):
        copy = pltpu.make_async_remote_copy(
            src_ref=full.at[mine], dst_ref=full.at[mine],
            send_sem=full_send.at[s], recv_sem=full_recv.at[s], device_id=shifted(0, s), device_id_type=MESH,
        )
        copy.start()
        copies.append(copy)
    for copy in copies:
        copy.wait()
    mass[...] = full[...]
    traces_copy.wait()

    everything = pl.ds(CAP, rows * 2 - CAP)
    pltpu.make_async_remote_copy(
        src_ref=out_rows.at[everything], dst_ref=out_rows.at[everything],
        send_sem=row_send, recv_sem=row_recv.at[0], device_id=(f, p), device_id_type=MESH,
    ).wait_send()
    assert sum(sent) % nodes == 0
    blocks = pl.ds(0, sum(sent) // nodes)
    pltpu.make_async_remote_copy(
        src_ref=gathered.at[blocks], dst_ref=gathered.at[blocks],
        send_sem=gather_send, recv_sem=gather_recv.at[0], device_id=(f, p), device_id_type=MESH,
    ).wait_send()


def finish(factor, traces, summed, traces_out, mass, sem):
    copy = pltpu.make_async_copy(traces, traces_out, sem)
    copy.start()
    wide = summed[...].astype(jnp.float32)
    mass[...] = (wide + wide.T) * factor
    copy.wait()


def shards(contributions, routes, slots, panels):
    rows, width = contributions.shape
    nodes = panels.shape[0]
    devices = lax.axis_size("fluid") * lax.axis_size("patch")
    bf16, f32, i32 = jnp.bfloat16, jnp.float32, jnp.int32
    strip = width // PLANE
    vmem, anywhere = pl.BlockSpec(memory_space=pltpu.VMEM), pl.BlockSpec(memory_space=pl.ANY)
    dma = pltpu.SemaphoreType.DMA
    summed = pl.pallas_call(
        kernel,
        out_shape=(
            jax.ShapeDtypeStruct((nodes, width), bf16),
            jax.ShapeDtypeStruct((width, width), bf16),
        ),
        in_specs=[anywhere, vmem, vmem, anywhere],
        out_specs=(anywhere, vmem),
        scratch_shapes=[
            pltpu.VMEM((rows, width), bf16),
            pltpu.VMEM((2 * rows, width), bf16),
            pltpu.VMEM((2 * rows, width), bf16),
            pltpu.VMEM((128, rows), bf16),
            pltpu.VMEM((1, rows), i32),
            pltpu.VMEM((128, 128), i32),
            pltpu.VMEM((COLUMN, PLANE, 128), i32),
            pltpu.VMEM((PLANE, 8, 128), i32),
            pltpu.VMEM((PLANE, 8, 128), i32),
            pltpu.VMEM((nodes, width), f32),
            pltpu.VMEM((PLANE, nodes, width), bf16),
            pltpu.VMEM((PLANE, nodes, nodes), bf16),
            pltpu.VMEM((nodes, width), f32),
            pltpu.VMEM((width, nodes), bf16),
            pltpu.VMEM((width, width), f32),
            pltpu.VMEM((width, width), bf16),
            pltpu.VMEM((PLANE, strip, width), bf16),
            pltpu.VMEM((COLUMN, strip, width), bf16),
            pltpu.VMEM((width, width), bf16),
            pltpu.SemaphoreType.REGULAR,
            dma, dma((PLANE,)), dma((COLUMN,)), dma((COLUMN,)), dma((PLANE,)), dma((PLANE,)),
            dma, dma((PLANE * 4,)), dma((PLANE,)),
            dma((2,)), dma((PLANE,)), dma((PLANE,)), dma((COLUMN,)), dma((COLUMN,)), dma((PLANE,)), dma((PLANE,)),
        ],
        compiler_params=pltpu.CompilerParams(
            collective_id=0, has_side_effects=True, vmem_limit_bytes=60 * 1024 * 1024
        ),
        cost_estimate=pl.CostEstimate(
            flops=2 * nodes * PLANE * nodes * width, bytes_accessed=nodes * nodes * PLANE * 2, transcendentals=0
        ),
    )(contributions, routes.reshape(1, rows), slots.reshape(1, rows), panels)
    return pl.pallas_call(
        functools.partial(finish, 0.5 / math.sqrt(nodes * devices)),
        out_shape=(
            jax.ShapeDtypeStruct((nodes, width), bf16),
            jax.ShapeDtypeStruct((width, width), f32),
        ),
        in_specs=[anywhere, vmem],
        out_specs=(anywhere, vmem),
        scratch_shapes=[dma],
    )(*summed)


def solution(mesh):
    placed = (
        P(("fluid", "patch"), None),
        P(("fluid", "patch"), None),
        P(("fluid", "patch")),
        P(("fluid", "patch"), None),
    )
    return jax.shard_map(
        shards,
        mesh=mesh,
        in_specs=placed,
        out_specs=(P(("fluid", "patch"), None), P()),
        check_vma=False,
    )
```

```python
import functools
import math

import jax
import jax.numpy as jnp
from jax import lax
from jax.experimental import pallas as pl
from jax.experimental.pallas import tpu as pltpu
from jax.sharding import PartitionSpec as P

MESH = pl.DeviceIdType.MESH
SIDE = 4
COLUMN = 8
PLANE = 16
CAP = 32
STRIDE = 5


def where_am_i():
    f, p = lax.axis_index("fluid"), lax.axis_index("patch")
    return f // 2, lax.rem(f, 2), p // SIDE, lax.rem(p, SIDE)


def shifted(column_step, plane_step, sign=1):
    z, c, x, y = where_am_i()
    dz, dc = column_step // 2, column_step % 2
    dx, dy = plane_step // SIDE, plane_step % SIDE
    if sign < 0:
        dz, dx, dy = SIDE - dz, SIDE - dx, SIDE - dy
    return (
        lax.rem(z + dz, SIDE) * 2 + lax.rem(c + dc, 2),
        lax.rem(x + dx, SIDE) * SIDE + lax.rem(y + dy, SIDE),
    )


def kernel(
    contributions_in, routes, slots, panels, traces, mass,
    contributions, out_rows, in_rows, onehot, position, slot_out, column_slots, plane_out, plane_slots, landed,
    gathered, panel_v, coupled, own_t, share, share_sent, reduce_in, column_in, full, entered,
    row_send, row_recv, slot_send, slot_recv, plane_send, plane_recv, gather_send, gather_recv, panel_sem,
    local_sem, reduce_send, reduce_recv, column_send, column_recv, full_send, full_recv,
):
    f32, bf16, i32 = jnp.float32, jnp.bfloat16, jnp.int32
    f, p = lax.axis_index("fluid"), lax.axis_index("patch")
    z, c, x, y = where_am_i()
    rows = contributions_in.shape[0]
    nodes = traces.shape[0]
    width = traces.shape[1]
    half, piece = nodes // 2, nodes // 4

    barrier = pltpu.get_barrier_semaphore()

    for s in range(1, PLANE):
        pl.semaphore_signal(barrier, inc=1, device_id=shifted(0, s), device_id_type=MESH)
    for w in range(1, COLUMN):
        pl.semaphore_signal(barrier, inc=1, device_id=shifted(w, 0), device_id_type=MESH)

    rows_copy = pltpu.make_async_copy(contributions_in, contributions, local_sem.at[0])
    rows_copy.start()

    to = routes[...]
    to_f, to_p = to >> 4, to & 15
    dz, dc = ((to_f >> 1) - z) & 3, ((to_f & 1) - c) & 1
    dx, dy = ((to_p >> 2) - x) & 3, ((to_p & 3) - y) & 3
    step_column, step_plane = dz * 2 + dc, dx * 4 + dy
    label = step_column * PLANE + step_plane
    onehot[...] = (lax.broadcasted_iota(i32, (128, rows), 0) == label).astype(bf16)
    block = 256
    pl.semaphore_wait(barrier, PLANE + COLUMN - 2)
    for w in range(1, COLUMN):
        pl.semaphore_signal(entered, inc=1, device_id=shifted(w, 0), device_id_type=MESH)

    upper = (
        lax.broadcasted_iota(i32, (block, block), 0) < lax.broadcasted_iota(i32, (block, block), 1)
    ).astype(bf16)
    seen = jnp.zeros((128, 1), f32)
    orders = []
    for b in range(rows // block):
        mine = onehot[:, b * block:(b + 1) * block]
        before = jnp.dot(mine, upper, preferred_element_type=f32) + seen
        wide = mine.astype(f32)
        orders.append(jnp.sum(wide * before, axis=0, keepdims=True))
        seen = seen + jnp.sum(wide, axis=1, keepdims=True)
    order = jnp.concatenate(orders, axis=1).astype(i32)
    turn = (step_plane - STRIDE * step_column) & 15
    position[...] = (turn * COLUMN + step_column) * CAP + order


    value = slots[...] + 1
    lane_order = lax.broadcasted_iota(i32, (128, rows), 0) & (CAP - 1)
    hit = lane_order == order
    nt = (((1,), (1,)), ((), ()))
    high = jnp.where(hit, (value >> 5).astype(f32), 0.0).astype(bf16)
    table = lax.dot_general(onehot[...], high, nt, preferred_element_type=f32) * 32.0
    low = jnp.where(hit, (value & 31).astype(f32), 0.0).astype(bf16)
    table = table + lax.dot_general(onehot[...], low, nt, preferred_element_type=f32)
    lane_group = lax.broadcasted_iota(i32, (128, 128), 1) >> 5
    row_group = (lax.broadcasted_iota(i32, (128, 128), 0) >> 4) & 3
    slot_out[...] = jnp.where(lane_group == row_group, table, 0.0).astype(i32)
    column_slots[0] = slot_out[0:PLANE]

    rows_copy.wait()
    pl.semaphore_wait(entered, COLUMN - 1)

    def build(kk):
        i = lax.broadcasted_iota(i32, (256, 1), 0)
        pick = (kk * 256 + i == position[...]).astype(bf16)
        made = jnp.dot(pick, contributions[...], preferred_element_type=f32).astype(bf16)
        out_rows[pl.ds(pl.multiple_of(kk * 256, 256), 256), :] = made

    def row_copy(kk, w):
        at = pl.ds(pl.multiple_of(kk * 256 + w * CAP, CAP), CAP)
        return pltpu.make_async_remote_copy(
            src_ref=out_rows.at[at], dst_ref=in_rows.at[at],
            send_sem=row_send, recv_sem=row_recv.at[kk],
            device_id=shifted(w, lax.rem(kk + STRIDE * w, PLANE)), device_id_type=MESH,
        )

    def send_rows(first, last):
        @pl.loop(first, last)
        def _(kk):
            build(kk)
            for w in range(COLUMN):
                row_copy(kk, w).start()

    slot_copies = []
    for w in range(1, COLUMN):
        copy = pltpu.make_async_remote_copy(
            src_ref=slot_out.at[pl.ds(w * PLANE, PLANE)], dst_ref=column_slots.at[w],
            send_sem=slot_send.at[w], recv_sem=slot_recv.at[w], device_id=shifted(w, 0), device_id_type=MESH,
        )
        copy.start()
        slot_copies.append(copy)

    send_rows(1, 4)

    for copy in slot_copies:
        copy.wait()
    first = column_slots[0] + column_slots[1] + column_slots[2] + column_slots[3]
    second = column_slots[4] + column_slots[5] + column_slots[6] + column_slots[7]
    sub = lax.broadcasted_iota(i32, (PLANE, 8, 128), 1)
    plane_out[...] = jnp.where(sub < 4, first[:, None, :], second[:, None, :])
    plane_slots[0] = plane_out[0]
    plane_copies = []
    for s in range(1, PLANE):
        copy = pltpu.make_async_remote_copy(
            src_ref=plane_out.at[s], dst_ref=plane_slots.at[s],
            send_sem=plane_send.at[s], recv_sem=plane_recv.at[s], device_id=shifted(0, s), device_id_type=MESH,
        )
        copy.start()
        plane_copies.append(copy)

    send_rows(4, PLANE)
    build(0)
    for w in range(1, COLUMN):
        row_copy(0, w).start()
    in_rows[0:CAP, :] = out_rows[0:CAP, :]

    panel_copies = []
    for s in range(PLANE):
        dx, dy = s // SIDE, s % SIDE
        owner = lax.rem(x + SIDE - dx, SIDE) * SIDE + lax.rem(y + SIDE - dy, SIDE)
        copy = pltpu.make_async_copy(
            panels.at[:, pl.ds(pl.multiple_of(owner * nodes, 128), nodes)], panel_v.at[s], panel_sem.at[s]
        )
        copy.start()
        panel_copies.append(copy)

    for copy in plane_copies:
        copy.wait()

    landed[...] = jnp.zeros_like(landed)

    def land(kk):
        group = lax.broadcasted_iota(i32, (1, 128), 1) >> 5
        parts = []
        for side in range(2):
            row = jnp.zeros((1, 128), i32)
            for k in range(4):
                w = side * 4 + k
                got = plane_slots[lax.rem(kk + STRIDE * w, PLANE), pl.ds(side * 4, 1), :]
                row = row + jnp.where(group == k, got, 0)
            parts.append(row)
        names = jnp.concatenate(parts, axis=1) - 1
        spread = (lax.broadcasted_iota(i32, (nodes, 256), 0) == names).astype(bf16)
        landed[...] += jnp.dot(
            spread, in_rows[pl.ds(pl.multiple_of(kk * 256, 256), 256), :], preferred_element_type=f32
        )

    def arrival(kk, start, count):
        at = pl.ds(start, count)
        return pltpu.make_async_remote_copy(
            src_ref=in_rows.at[at], dst_ref=in_rows.at[at],
            send_sem=row_send, recv_sem=row_recv.at[kk], device_id=(f, p), device_id_type=MESH,
        )

    @pl.loop(1, PLANE)
    def _(kk):
        arrival(kk, pl.multiple_of(kk * 256, 256), 256).wait_recv()
        land(kk)

    arrival(0, CAP, 256 - CAP).wait_recv()
    land(0)
    own = landed[...].astype(bf16)
    gathered[0] = own

    sent = []

    def pass_on(axis, direction, source, start, count, sem):
        dx, dy = source
        if axis == 0:
            dx = (dx + direction) % SIDE
            device = (f, lax.rem(x + direction + SIDE, SIDE) * SIDE + y)
        else:
            dy = (dy + direction) % SIDE
            device = (f, x * SIDE + lax.rem(y + direction + SIDE, SIDE))
        at = pl.ds(start, count)
        copy = pltpu.make_async_remote_copy(
            src_ref=gathered.at[source[0] * SIDE + source[1], at], dst_ref=gathered.at[dx * SIDE + dy, at],
            send_sem=gather_send, recv_sem=gather_recv.at[(dx * SIDE + dy) * 4 + sem],
            device_id=device, device_id_type=MESH,
        )
        copy.start()
        sent.append(count)

    def await_piece(source, start, count, sem):
        s = source[0] * SIDE + source[1]
        at = pl.ds(start, count)
        pltpu.make_async_remote_copy(
            src_ref=gathered.at[s, at], dst_ref=gathered.at[s, at],
            send_sem=gather_send, recv_sem=gather_recv.at[s * 4 + sem], device_id=(f, p), device_id_type=MESH,
        ).wait_recv()

    def at(lead, a, b):
        return (a, b) if lead == 0 else (b, a)

    def send_half(lead, axis, direction, source):
        pass_on(axis, direction, source, lead * half, half, lead * 2)

    def send_piece(lead, axis, direction, source, k):
        pass_on(axis, direction, source, lead * half + k * piece, piece, lead * 2 + k)

    def wait_half(lead, source):
        await_piece(source, lead * half, half, lead * 2)

    def wait_piece(lead, source, k):
        await_piece(source, lead * half + k * piece, piece, lead * 2 + k)

    def multiply(s, start, count):
        coupled[...] += jnp.dot(
            panel_v[s, :, pl.ds(start, count)], gathered[s, pl.ds(start, count), :], preferred_element_type=f32
        )

    for turned in (0, 1):
        for direction in (1, -1):
            for lead in (0, 1):
                send_half(lead, lead ^ turned, direction, (0, 0))
    traces_copy = pltpu.make_async_copy(gathered.at[0], traces, local_sem.at[1])
    traces_copy.start()
    own_t[...] = own.T
    coupled[...] = jnp.zeros_like(coupled)
    for copy in panel_copies:
        copy.wait()
    multiply(0, 0, nodes)

    def multiply_halves(places):
        for lead, place in places:
            multiply(place[0] * SIDE + place[1], lead * half, half)

    for k, a, direction in ((0, 1, 1), (1, 3, -1)):
        for lead in (0, 1):
            place = at(lead, a, 0)
            wait_half(lead, place)
            send_piece(lead, lead, direction, place, k)
            send_half(lead, 1 - lead, 1, place)
            send_half(lead, 1 - lead, -1, place)
    multiply_halves([(lead, at(lead, a, 0)) for a in (1, 3) for lead in (0, 1)])
    for k in (0, 1):
        for lead in (0, 1):
            place = at(lead, 2, 0)
            wait_piece(lead, place, k)
            send_piece(lead, 1 - lead, 1, place, k)
            send_piece(lead, 1 - lead, -1, place, k)
    for k, b, direction in ((0, 1, 1), (1, 3, -1)):
        for lead in (0, 1):
            place = at(lead, 0, b)
            wait_half(lead, place)
            send_piece(lead, 1 - lead, direction, place, k)
    multiply_halves([(lead, at(lead, a, b)) for a, b in ((2, 0), (0, 1), (0, 3)) for lead in (0, 1)])
    for a in (1, 3):
        for k, b, direction in ((0, 1, 1), (1, 3, -1)):
            for lead in (0, 1):
                place = at(lead, a, b)
                wait_half(lead, place)
                send_piece(lead, 1 - lead, direction, place, k)
        multiply_halves([(lead, at(lead, a, b)) for b in (1, 3) for lead in (0, 1)])
    for k in (0, 1):
        for lead in (0, 1):
            wait_piece(lead, at(lead, 0, 2), k)
    multiply_halves([(lead, at(lead, 0, 2)) for lead in (0, 1)])
    for lead in (0, 1):
        place = at(lead, 2, 1)
        wait_piece(lead, place, 0)
        send_piece(lead, 1 - lead, 1, place, 0)
        place = at(lead, 2, 3)
        wait_piece(lead, place, 1)
        send_piece(lead, 1 - lead, -1, place, 1)
    for lead in (0, 1):
        wait_piece(lead, at(lead, 2, 1), 1)
        wait_piece(lead, at(lead, 2, 3), 0)
    multiply_halves([(lead, at(lead, 2, b)) for b in (1, 3) for lead in (0, 1)])
    for a in (1, 3):
        for k in (0, 1):
            for lead in (0, 1):
                wait_piece(lead, at(lead, a, 2), k)
        multiply_halves([(lead, at(lead, a, 2)) for lead in (0, 1)])
    for k in (0, 1):
        for lead in (0, 1):
            wait_piece(lead, at(lead, 2, 2), k)
    multiply_halves([(lead, at(lead, 2, 2)) for lead in (0, 1)])

    top = coupled[...].astype(bf16)
    rest = (coupled[...] - top.astype(f32)).astype(bf16)
    share[...] = jnp.dot(own_t[...], top, preferred_element_type=f32) + jnp.dot(
        own_t[...], rest, preferred_element_type=f32
    )
    share_sent[...] = share[...].astype(bf16)

    strip = width // PLANE
    copies = []
    for s in range(1, PLANE):
        device = shifted(0, s)
        copy = pltpu.make_async_remote_copy(
            src_ref=share_sent.at[pl.ds(pl.multiple_of(device[1] * strip, strip), strip)], dst_ref=reduce_in.at[s],
            send_sem=reduce_send.at[s], recv_sem=reduce_recv.at[s], device_id=device, device_id_type=MESH,
        )
        copy.start()
        copies.append(copy)
    mine = pl.ds(pl.multiple_of(p * strip, strip), strip)
    total = share[mine, :]
    for s, copy in enumerate(copies):
        copy.wait()
        total = total + reduce_in[s + 1].astype(f32)
    column_in[f] = total.astype(bf16)
    copies = []
    for w in range(1, COLUMN):
        copy = pltpu.make_async_remote_copy(
            src_ref=column_in.at[f], dst_ref=column_in.at[f],
            send_sem=column_send.at[w], recv_sem=column_recv.at[w], device_id=shifted(w, 0), device_id_type=MESH,
        )
        copy.start()
        copies.append(copy)
    for copy in copies:
        copy.wait()
    total = column_in[0].astype(f32)
    for w in range(1, COLUMN):
        total = total + column_in[w].astype(f32)
    full[mine, :] = total.astype(bf16)
    copies = []
    for s in range(1, PLANE):
        copy = pltpu.make_async_remote_copy(
            src_ref=full.at[mine], dst_ref=full.at[mine],
            send_sem=full_send.at[s], recv_sem=full_recv.at[s], device_id=shifted(0, s), device_id_type=MESH,
        )
        copy.start()
        copies.append(copy)
    for copy in copies:
        copy.wait()
    mass[...] = full[...]
    traces_copy.wait()

    everything = pl.ds(CAP, rows * 2 - CAP)
    pltpu.make_async_remote_copy(
        src_ref=out_rows.at[everything], dst_ref=out_rows.at[everything],
        send_sem=row_send, recv_sem=row_recv.at[0], device_id=(f, p), device_id_type=MESH,
    ).wait_send()
    assert sum(sent) % nodes == 0
    blocks = pl.ds(0, sum(sent) // nodes)
    pltpu.make_async_remote_copy(
        src_ref=gathered.at[blocks], dst_ref=gathered.at[blocks],
        send_sem=gather_send, recv_sem=gather_recv.at[0], device_id=(f, p), device_id_type=MESH,
    ).wait_send()


def finish(factor, traces, summed, traces_out, mass):
    traces_out[...] = traces[...]
    wide = summed[...].astype(jnp.float32)
    mass[...] = (wide + wide.T) * factor


def shards(contributions, routes, slots, panels):
    rows, width = contributions.shape
    nodes = panels.shape[0]
    devices = lax.axis_size("fluid") * lax.axis_size("patch")
    bf16, f32, i32 = jnp.bfloat16, jnp.float32, jnp.int32
    strip = width // PLANE
    vmem, anywhere = pl.BlockSpec(memory_space=pltpu.VMEM), pl.BlockSpec(memory_space=pl.ANY)
    dma = pltpu.SemaphoreType.DMA
    summed = pl.pallas_call(
        kernel,
        out_shape=(
            jax.ShapeDtypeStruct((nodes, width), bf16),
            jax.ShapeDtypeStruct((width, width), bf16),
        ),
        in_specs=[anywhere, vmem, vmem, anywhere],
        out_specs=(anywhere, vmem),
        scratch_shapes=[
            pltpu.VMEM((rows, width), bf16),
            pltpu.VMEM((2 * rows, width), bf16),
            pltpu.VMEM((2 * rows, width), bf16),
            pltpu.VMEM((128, rows), bf16),
            pltpu.VMEM((1, rows), i32),
            pltpu.VMEM((128, 128), i32),
            pltpu.VMEM((COLUMN, PLANE, 128), i32),
            pltpu.VMEM((PLANE, 8, 128), i32),
            pltpu.VMEM((PLANE, 8, 128), i32),
            pltpu.VMEM((nodes, width), f32),
            pltpu.VMEM((PLANE, nodes, width), bf16),
            pltpu.VMEM((PLANE, nodes, nodes), bf16),
            pltpu.VMEM((nodes, width), f32),
            pltpu.VMEM((width, nodes), bf16),
            pltpu.VMEM((width, width), f32),
            pltpu.VMEM((width, width), bf16),
            pltpu.VMEM((PLANE, strip, width), bf16),
            pltpu.VMEM((COLUMN, strip, width), bf16),
            pltpu.VMEM((width, width), bf16),
            pltpu.SemaphoreType.REGULAR,
            dma, dma((PLANE,)), dma((COLUMN,)), dma((COLUMN,)), dma((PLANE,)), dma((PLANE,)),
            dma, dma((PLANE * 4,)), dma((PLANE,)),
            dma((2,)), dma((PLANE,)), dma((PLANE,)), dma((COLUMN,)), dma((COLUMN,)), dma((PLANE,)), dma((PLANE,)),
        ],
        compiler_params=pltpu.CompilerParams(
            collective_id=0, has_side_effects=True, vmem_limit_bytes=60 * 1024 * 1024
        ),
        cost_estimate=pl.CostEstimate(
            flops=2 * nodes * PLANE * nodes * width, bytes_accessed=nodes * nodes * PLANE * 2, transcendentals=0
        ),
    )(contributions, routes.reshape(1, rows), slots.reshape(1, rows), panels)
    return pl.pallas_call(
        functools.partial(finish, 0.5 / math.sqrt(nodes * devices)),
        out_shape=(
            jax.ShapeDtypeStruct((nodes, width), bf16),
            jax.ShapeDtypeStruct((width, width), f32),
        ),
        in_specs=[vmem, vmem],
        out_specs=(vmem, vmem),
    )(*summed)


def solution(mesh):
    placed = (
        P(("fluid", "patch"), None),
        P(("fluid", "patch"), None),
        P(("fluid", "patch")),
        P(("fluid", "patch"), None),
    )
    return jax.shard_map(
        shards,
        mesh=mesh,
        in_specs=placed,
        out_specs=(P(("fluid", "patch"), None), P()),
        check_vma=False,
    )
```

```python
import functools
import math

import jax
import jax.numpy as jnp
from jax import lax
from jax.experimental import pallas as pl
from jax.experimental.pallas import tpu as pltpu
from jax.sharding import PartitionSpec as P

MESH = pl.DeviceIdType.MESH
SIDE = 4
COLUMN = 8
PLANE = 16
CAP = 32
SLOT_BITS = 10
STRIDE = 5
PLANE_PEERS = (10, 9, 11, 6, 14, 2, 8, 5, 7, 13, 15, 1, 3, 4, 12)
COLUMN_PEERS = (5, 4, 3, 7, 2, 6, 1)


def where_am_i():
    f, p = lax.axis_index("fluid"), lax.axis_index("patch")
    return f // 2, lax.rem(f, 2), p // SIDE, lax.rem(p, SIDE)


def shifted(column_step, plane_step, sign=1):
    z, c, x, y = where_am_i()
    dz, dc = column_step // 2, column_step % 2
    dx, dy = plane_step // SIDE, plane_step % SIDE
    if sign < 0:
        dz, dx, dy = SIDE - dz, SIDE - dx, SIDE - dy
    return (
        lax.rem(z + dz, SIDE) * 2 + lax.rem(c + dc, 2),
        lax.rem(x + dx, SIDE) * SIDE + lax.rem(y + dy, SIDE),
    )


def kernel(
    contributions_in, names_in, panels, traces, mass,
    contributions, out_rows, in_rows, onehot, position, slot_out, column_slots, plane_out, plane_slots, landed,
    gathered, panel_v, coupled, own_t, share, share_sent, reduce_in, column_in, full, entered,
    row_send, row_recv, slot_send, slot_recv, plane_send, plane_recv, gather_send, gather_recv, panel_sem,
    operand_sem, local_sem, reduce_send, reduce_recv, column_send, column_recv, full_send, full_recv,
):
    f32, bf16, i32 = jnp.float32, jnp.bfloat16, jnp.int32
    f, p = lax.axis_index("fluid"), lax.axis_index("patch")
    z, c, x, y = where_am_i()
    rows = contributions_in.shape[0]
    nodes = traces.shape[0]
    width = traces.shape[1]
    half, piece = nodes // 2, nodes // 4

    rows_copy = pltpu.make_async_copy(contributions_in, contributions, operand_sem)
    rows_copy.start()

    barrier = pltpu.get_barrier_semaphore()

    for s in PLANE_PEERS:
        pl.semaphore_signal(barrier, inc=1, device_id=shifted(0, s), device_id_type=MESH)
    for w in COLUMN_PEERS:
        pl.semaphore_signal(barrier, inc=1, device_id=shifted(w, 0), device_id_type=MESH)

    to = names_in[...] >> SLOT_BITS
    to_f, to_p = to >> 4, to & 15
    dz, dc = ((to_f >> 1) - z) & 3, ((to_f & 1) - c) & 1
    dx, dy = ((to_p >> 2) - x) & 3, ((to_p & 3) - y) & 3
    step_column, step_plane = dz * 2 + dc, dx * 4 + dy
    label = step_column * PLANE + step_plane
    onehot[...] = (lax.broadcasted_iota(i32, (128, rows), 0) == label).astype(bf16)
    block = 256
    pl.semaphore_wait(barrier, PLANE + COLUMN - 2)
    for w in COLUMN_PEERS:
        pl.semaphore_signal(entered, inc=1, device_id=shifted(w, 0), device_id_type=MESH)

    upper = (
        lax.broadcasted_iota(i32, (block, block), 0) < lax.broadcasted_iota(i32, (block, block), 1)
    ).astype(bf16)
    seen = jnp.zeros((128, 1), f32)
    orders = []
    for b in range(rows // block):
        mine = onehot[:, b * block:(b + 1) * block]
        before = jnp.dot(mine, upper, preferred_element_type=f32) + seen
        wide = mine.astype(f32)
        orders.append(jnp.sum(wide * before, axis=0, keepdims=True))
        seen = seen + jnp.sum(wide, axis=1, keepdims=True)
    order = jnp.concatenate(orders, axis=1).astype(i32)
    turn = (step_plane - STRIDE * step_column) & 15
    position[...] = (turn * COLUMN + step_column) * CAP + order

    value = (names_in[...] & ((1 << SLOT_BITS) - 1)) + 1
    lane_order = lax.broadcasted_iota(i32, (128, rows), 0) & (CAP - 1)
    hit = lane_order == order
    nt = (((1,), (1,)), ((), ()))
    high = jnp.where(hit, (value >> 5).astype(f32), 0.0).astype(bf16)
    table = lax.dot_general(onehot[...], high, nt, preferred_element_type=f32) * 32.0
    low = jnp.where(hit, (value & 31).astype(f32), 0.0).astype(bf16)
    table = table + lax.dot_general(onehot[...], low, nt, preferred_element_type=f32)
    lane_group = lax.broadcasted_iota(i32, (128, 128), 1) >> 5
    row_group = (lax.broadcasted_iota(i32, (128, 128), 0) >> 4) & 3
    slot_out[...] = jnp.where(lane_group == row_group, table, 0.0).astype(i32)
    column_slots[0] = slot_out[0:PLANE]

    rows_copy.wait()

    def picked(rows_wanted):
        pick = (rows_wanted == position[...]).astype(bf16)
        return jnp.dot(pick, contributions[...], preferred_element_type=f32).astype(bf16)

    def build_plane(first):
        i = lax.broadcasted_iota(i32, (256, 1), 0)
        made = picked((first + (i >> 5)) * 256 + (i & 31))
        for k in range(8):
            out_rows[(first + k) * 256:(first + k) * 256 + CAP, :] = made[k * CAP:(k + 1) * CAP]

    def build(kk):
        i = lax.broadcasted_iota(i32, (256 - CAP, 1), 0)
        out_rows[pl.ds(pl.multiple_of(kk * 256 + CAP, CAP), 256 - CAP), :] = picked(kk * 256 + CAP + i)

    def row_copy(kk, w):
        at = pl.ds(pl.multiple_of(kk * 256 + w * CAP, CAP), CAP)
        return pltpu.make_async_remote_copy(
            src_ref=out_rows.at[at], dst_ref=in_rows.at[at],
            send_sem=row_send, recv_sem=row_recv.at[kk],
            device_id=shifted(w, lax.rem(kk + STRIDE * w, PLANE)), device_id_type=MESH,
        )

    def send_rows(first, last):
        @pl.loop(first, last)
        def _(kk):
            build(kk)
            for w in range(1, COLUMN):
                row_copy(kk, w).start()

    slot_copies = []
    for w in COLUMN_PEERS:
        copy = pltpu.make_async_remote_copy(
            src_ref=slot_out.at[pl.ds(w * PLANE, PLANE)], dst_ref=column_slots.at[w],
            send_sem=slot_send.at[w], recv_sem=slot_recv.at[w], device_id=shifted(w, 0), device_id_type=MESH,
        )
        copy.start()
        slot_copies.append(copy)

    for first in (8, 0):
        build_plane(first)
        for kk in range(first, first + 8):
            if kk > 0:
                row_copy(kk, 0).start()

    pl.semaphore_wait(entered, COLUMN - 1)
    send_rows(1, 4)

    for copy in slot_copies:
        copy.wait()
    first = column_slots[0] + column_slots[1] + column_slots[2] + column_slots[3]
    second = column_slots[4] + column_slots[5] + column_slots[6] + column_slots[7]
    sub = lax.broadcasted_iota(i32, (PLANE, 8, 128), 1)
    plane_out[...] = jnp.where(sub < 4, first[:, None, :], second[:, None, :])
    plane_slots[0] = plane_out[0]
    plane_copies = []
    for s in PLANE_PEERS:
        copy = pltpu.make_async_remote_copy(
            src_ref=plane_out.at[s], dst_ref=plane_slots.at[s],
            send_sem=plane_send.at[s], recv_sem=plane_recv.at[s], device_id=shifted(0, s), device_id_type=MESH,
        )
        copy.start()
        plane_copies.append(copy)

    send_rows(4, PLANE)
    build(0)
    for w in range(1, COLUMN):
        row_copy(0, w).start()
    in_rows[0:CAP, :] = out_rows[0:CAP, :]

    panel_copies = []
    for s in range(PLANE):
        dx, dy = s // SIDE, s % SIDE
        owner = lax.rem(x + SIDE - dx, SIDE) * SIDE + lax.rem(y + SIDE - dy, SIDE)
        copy = pltpu.make_async_copy(
            panels.at[:, pl.ds(pl.multiple_of(owner * nodes, 128), nodes)], panel_v.at[s], panel_sem.at[s]
        )
        copy.start()
        panel_copies.append(copy)

    for copy in plane_copies:
        copy.wait()

    landed[...] = jnp.zeros_like(landed)

    def land(kk):
        group = lax.broadcasted_iota(i32, (1, 128), 1) >> 5
        parts = []
        for side in range(2):
            row = jnp.zeros((1, 128), i32)
            for k in range(4):
                w = side * 4 + k
                got = plane_slots[lax.rem(kk + STRIDE * w, PLANE), pl.ds(side * 4, 1), :]
                row = row + jnp.where(group == k, got, 0)
            parts.append(row)
        names = jnp.concatenate(parts, axis=1) - 1
        spread = (lax.broadcasted_iota(i32, (nodes, 256), 0) == names).astype(bf16)
        landed[...] += jnp.dot(
            spread, in_rows[pl.ds(pl.multiple_of(kk * 256, 256), 256), :], preferred_element_type=f32
        )

    def arrival(kk, start, count):
        at = pl.ds(start, count)
        return pltpu.make_async_remote_copy(
            src_ref=in_rows.at[at], dst_ref=in_rows.at[at],
            send_sem=row_send, recv_sem=row_recv.at[kk], device_id=(f, p), device_id_type=MESH,
        )

    @pl.loop(1, PLANE)
    def _(kk):
        arrival(kk, pl.multiple_of(kk * 256, 256), 256).wait_recv()
        land(kk)

    arrival(0, CAP, 256 - CAP).wait_recv()
    land(0)
    own = landed[...].astype(bf16)
    gathered[0] = own

    sent = []

    def pass_on(axis, direction, source, start, count, sem):
        dx, dy = source
        if axis == 0:
            dx = (dx + direction) % SIDE
            device = (f, lax.rem(x + direction + SIDE, SIDE) * SIDE + y)
        else:
            dy = (dy + direction) % SIDE
            device = (f, x * SIDE + lax.rem(y + direction + SIDE, SIDE))
        at = pl.ds(start, count)
        copy = pltpu.make_async_remote_copy(
            src_ref=gathered.at[source[0] * SIDE + source[1], at], dst_ref=gathered.at[dx * SIDE + dy, at],
            send_sem=gather_send, recv_sem=gather_recv.at[(dx * SIDE + dy) * 4 + sem],
            device_id=device, device_id_type=MESH,
        )
        copy.start()
        sent.append(count)

    def await_piece(source, start, count, sem):
        s = source[0] * SIDE + source[1]
        at = pl.ds(start, count)
        pltpu.make_async_remote_copy(
            src_ref=gathered.at[s, at], dst_ref=gathered.at[s, at],
            send_sem=gather_send, recv_sem=gather_recv.at[s * 4 + sem], device_id=(f, p), device_id_type=MESH,
        ).wait_recv()

    def at(lead, a, b):
        return (a, b) if lead == 0 else (b, a)

    def send_half(lead, axis, direction, source):
        pass_on(axis, direction, source, lead * half, half, lead * 2)

    def send_piece(lead, axis, direction, source, k):
        pass_on(axis, direction, source, lead * half + k * piece, piece, lead * 2 + k)

    def wait_half(lead, source):
        await_piece(source, lead * half, half, lead * 2)

    def wait_piece(lead, source, k):
        await_piece(source, lead * half + k * piece, piece, lead * 2 + k)

    def multiply(s, start, count):
        coupled[...] += jnp.dot(
            panel_v[s, :, pl.ds(start, count)], gathered[s, pl.ds(start, count), :], preferred_element_type=f32
        )

    for turned in (0, 1):
        for direction in (1, -1):
            for lead in (0, 1):
                send_half(lead, lead ^ turned, direction, (0, 0))
    traces_copy = pltpu.make_async_copy(gathered.at[0], traces, local_sem)
    traces_copy.start()
    own_t[...] = own.T
    coupled[...] = jnp.zeros_like(coupled)
    for copy in panel_copies:
        copy.wait()
    multiply(0, 0, nodes)

    def multiply_halves(places):
        for lead, place in places:
            multiply(place[0] * SIDE + place[1], lead * half, half)

    for k, a, direction in ((0, 1, 1), (1, 3, -1)):
        for lead in (0, 1):
            place = at(lead, a, 0)
            wait_half(lead, place)
            send_piece(lead, lead, direction, place, k)
            send_half(lead, 1 - lead, 1, place)
            send_half(lead, 1 - lead, -1, place)
    multiply_halves([(lead, at(lead, a, 0)) for a in (1, 3) for lead in (0, 1)])
    for k in (0, 1):
        for lead in (0, 1):
            place = at(lead, 2, 0)
            wait_piece(lead, place, k)
            send_piece(lead, 1 - lead, 1, place, k)
            send_piece(lead, 1 - lead, -1, place, k)
    for k, b, direction in ((0, 1, 1), (1, 3, -1)):
        for lead in (0, 1):
            place = at(lead, 0, b)
            wait_half(lead, place)
            send_piece(lead, 1 - lead, direction, place, k)
    multiply_halves([(lead, at(lead, a, b)) for a, b in ((2, 0), (0, 1), (0, 3)) for lead in (0, 1)])
    for a in (1, 3):
        for k, b, direction in ((0, 1, 1), (1, 3, -1)):
            for lead in (0, 1):
                place = at(lead, a, b)
                wait_half(lead, place)
                send_piece(lead, 1 - lead, direction, place, k)
        multiply_halves([(lead, at(lead, a, b)) for b in (1, 3) for lead in (0, 1)])
    for k in (0, 1):
        for lead in (0, 1):
            wait_piece(lead, at(lead, 0, 2), k)
    multiply_halves([(lead, at(lead, 0, 2)) for lead in (0, 1)])
    for lead in (0, 1):
        place = at(lead, 2, 1)
        wait_piece(lead, place, 0)
        send_piece(lead, 1 - lead, 1, place, 0)
        place = at(lead, 2, 3)
        wait_piece(lead, place, 1)
        send_piece(lead, 1 - lead, -1, place, 1)
    for lead in (0, 1):
        wait_piece(lead, at(lead, 2, 1), 1)
        wait_piece(lead, at(lead, 2, 3), 0)
    multiply_halves([(lead, at(lead, 2, b)) for b in (1, 3) for lead in (0, 1)])
    for a in (1, 3):
        for k in (0, 1):
            for lead in (0, 1):
                wait_piece(lead, at(lead, a, 2), k)
        multiply_halves([(lead, at(lead, a, 2)) for lead in (0, 1)])
    for k in (0, 1):
        for lead in (0, 1):
            wait_piece(lead, at(lead, 2, 2), k)

    last = 2 * SIDE + 2
    total = jnp.zeros((width, width), f32)
    for r in range(0, nodes, 256):
        wide = coupled[r:r + 256, :] + jnp.dot(
            panel_v[last, r:r + 256, :], gathered[last], preferred_element_type=f32
        )
        top = wide.astype(bf16)
        rest = (wide - top.astype(f32)).astype(bf16)
        left = own_t[:, r:r + 256]
        total = total + jnp.dot(left, top, preferred_element_type=f32)
        total = total + jnp.dot(left, rest, preferred_element_type=f32)
    share[...] = total
    share_sent[...] = share[...].astype(bf16)

    strip = width // PLANE
    copies = []
    for s in PLANE_PEERS:
        device = shifted(0, s)
        copy = pltpu.make_async_remote_copy(
            src_ref=share_sent.at[pl.ds(pl.multiple_of(device[1] * strip, strip), strip)], dst_ref=reduce_in.at[s],
            send_sem=reduce_send.at[s], recv_sem=reduce_recv.at[s], device_id=device, device_id_type=MESH,
        )
        copy.start()
        copies.append(copy)
    mine = pl.ds(pl.multiple_of(p * strip, strip), strip)
    total = share[mine, :]
    for copy in copies:
        copy.wait()
    for s in range(1, PLANE):
        total = total + reduce_in[s].astype(f32)
    column_in[f] = total.astype(bf16)
    copies = []
    for w in COLUMN_PEERS:
        copy = pltpu.make_async_remote_copy(
            src_ref=column_in.at[f], dst_ref=column_in.at[f],
            send_sem=column_send.at[w], recv_sem=column_recv.at[w], device_id=shifted(w, 0), device_id_type=MESH,
        )
        copy.start()
        copies.append(copy)
    for copy in copies:
        copy.wait()
    total = column_in[0].astype(f32)
    for w in range(1, COLUMN):
        total = total + column_in[w].astype(f32)
    full[mine, :] = total.astype(bf16)
    copies = []
    for s in PLANE_PEERS:
        copy = pltpu.make_async_remote_copy(
            src_ref=full.at[mine], dst_ref=full.at[mine],
            send_sem=full_send.at[s], recv_sem=full_recv.at[s], device_id=shifted(0, s), device_id_type=MESH,
        )
        copy.start()
        copies.append(copy)
    for copy in copies:
        copy.wait()
    mass[...] = full[...]
    traces_copy.wait()

    everything = pl.ds(CAP, rows * 2 - CAP)
    pltpu.make_async_remote_copy(
        src_ref=out_rows.at[everything], dst_ref=out_rows.at[everything],
        send_sem=row_send, recv_sem=row_recv.at[0], device_id=(f, p), device_id_type=MESH,
    ).wait_send()
    assert sum(sent) % nodes == 0
    blocks = pl.ds(0, sum(sent) // nodes)
    pltpu.make_async_remote_copy(
        src_ref=gathered.at[blocks], dst_ref=gathered.at[blocks],
        send_sem=gather_send, recv_sem=gather_recv.at[0], device_id=(f, p), device_id_type=MESH,
    ).wait_send()


def finish(factor, traces, summed, traces_out, mass):
    traces_out[...] = traces[...]
    wide = summed[...].astype(jnp.float32)
    mass[...] = (wide + wide.T) * factor


def shards(contributions, routes, slots, panels):
    rows, width = contributions.shape
    nodes = panels.shape[0]
    devices = lax.axis_size("fluid") * lax.axis_size("patch")
    bf16, f32, i32 = jnp.bfloat16, jnp.float32, jnp.int32
    strip = width // PLANE
    vmem, anywhere = pl.BlockSpec(memory_space=pltpu.VMEM), pl.BlockSpec(memory_space=pl.ANY)
    hbm = pl.BlockSpec(memory_space=pltpu.HBM)
    dma = pltpu.SemaphoreType.DMA
    names = (routes * (1 << SLOT_BITS) + slots.reshape(rows, 1)).reshape(1, rows)
    summed = pl.pallas_call(
        kernel,
        out_shape=(
            jax.ShapeDtypeStruct((nodes, width), bf16),
            jax.ShapeDtypeStruct((width, width), bf16),
        ),
        in_specs=[hbm, vmem, hbm],
        out_specs=(anywhere, vmem),
        scratch_shapes=[
            pltpu.VMEM((rows, width), bf16),
            pltpu.VMEM((2 * rows, width), bf16),
            pltpu.VMEM((2 * rows, width), bf16),
            pltpu.VMEM((128, rows), bf16),
            pltpu.VMEM((1, rows), i32),
            pltpu.VMEM((128, 128), i32),
            pltpu.VMEM((COLUMN, PLANE, 128), i32),
            pltpu.VMEM((PLANE, 8, 128), i32),
            pltpu.VMEM((PLANE, 8, 128), i32),
            pltpu.VMEM((nodes, width), f32),
            pltpu.VMEM((PLANE, nodes, width), bf16),
            pltpu.VMEM((PLANE, nodes, nodes), bf16),
            pltpu.VMEM((nodes, width), f32),
            pltpu.VMEM((width, nodes), bf16),
            pltpu.VMEM((width, width), f32),
            pltpu.VMEM((width, width), bf16),
            pltpu.VMEM((PLANE, strip, width), bf16),
            pltpu.VMEM((COLUMN, strip, width), bf16),
            pltpu.VMEM((width, width), bf16),
            pltpu.SemaphoreType.REGULAR,
            dma, dma((PLANE,)), dma((COLUMN,)), dma((COLUMN,)), dma((PLANE,)), dma((PLANE,)),
            dma, dma((PLANE * 4,)), dma((PLANE,)),
            dma, dma, dma((PLANE,)), dma((PLANE,)), dma((COLUMN,)), dma((COLUMN,)), dma((PLANE,)), dma((PLANE,)),
        ],
        compiler_params=pltpu.CompilerParams(
            collective_id=0, has_side_effects=True, vmem_limit_bytes=53 * 1024 * 1024
        ),
        cost_estimate=pl.CostEstimate(
            flops=2 * nodes * PLANE * nodes * width, bytes_accessed=nodes * nodes * PLANE * 2, transcendentals=0
        ),
    )(contributions, names, panels)
    return pl.pallas_call(
        functools.partial(finish, 0.5 / math.sqrt(nodes * devices)),
        out_shape=(
            jax.ShapeDtypeStruct((nodes, width), bf16),
            jax.ShapeDtypeStruct((width, width), f32),
        ),
        in_specs=[vmem, vmem],
        out_specs=(vmem, vmem),
        compiler_params=pltpu.CompilerParams(vmem_limit_bytes=4 * 1024 * 1024),
    )(*summed)


def solution(mesh):
    placed = (
        P(("fluid", "patch"), None),
        P(("fluid", "patch"), None),
        P(("fluid", "patch")),
        P(("fluid", "patch"), None),
    )
    return jax.shard_map(
        shards,
        mesh=mesh,
        in_specs=placed,
        out_specs=(P(("fluid", "patch"), None), P()),
        check_vma=False,
    )
```

```python
import functools
import math

import jax
import jax.numpy as jnp
from jax import lax
from jax.experimental import pallas as pl
from jax.experimental.pallas import tpu as pltpu
from jax.sharding import PartitionSpec as P

MESH = pl.DeviceIdType.MESH
SIDE = 4
COLUMN = 8
PLANE = 16
CAP = 32
SLOT_BITS = 10
STRIDE = 7
PLANE_PEERS = (10, 9, 11, 6, 14, 2, 8, 5, 7, 13, 15, 1, 3, 4, 12)
COLUMN_PEERS = (5, 4, 3, 7, 2, 6, 1)


def where_am_i():
    f, p = lax.axis_index("fluid"), lax.axis_index("patch")
    return f // 2, lax.rem(f, 2), p // SIDE, lax.rem(p, SIDE)


def shifted(column_step, plane_step, sign=1):
    z, c, x, y = where_am_i()
    dz, dc = column_step // 2, column_step % 2
    dx, dy = plane_step // SIDE, plane_step % SIDE
    if sign < 0:
        dz, dx, dy = SIDE - dz, SIDE - dx, SIDE - dy
    return (
        lax.rem(z + dz, SIDE) * 2 + lax.rem(c + dc, 2),
        lax.rem(x + dx, SIDE) * SIDE + lax.rem(y + dy, SIDE),
    )


def plane_step_of(turn, w):
    if isinstance(turn, int) and turn == 0:
        return 0
    return lax.rem(turn - 1 + STRIDE * w % (PLANE - 1), PLANE - 1) + 1


def kernel(
    contributions_in, names_in, panels, traces, mass,
    contributions, out_rows, in_rows, onehot, position, slot_out, column_slots, plane_out, plane_slots, landed,
    gathered, panel_v, coupled, own_t, share, share_sent, reduce_in, column_in, full, entered,
    row_send, row_recv, slot_send, slot_recv, plane_send, plane_recv, gather_send, gather_recv, panel_sem,
    operand_sem, local_sem, reduce_send, reduce_recv, column_send, column_recv, full_send, full_recv,
):
    f32, bf16, i32 = jnp.float32, jnp.bfloat16, jnp.int32
    f, p = lax.axis_index("fluid"), lax.axis_index("patch")
    z, c, x, y = where_am_i()
    rows = contributions_in.shape[0]
    nodes = traces.shape[0]
    width = traces.shape[1]
    half, piece = nodes // 2, nodes // 4

    rows_copy = pltpu.make_async_copy(contributions_in, contributions, operand_sem)
    rows_copy.start()

    barrier = pltpu.get_barrier_semaphore()

    for s in PLANE_PEERS:
        pl.semaphore_signal(barrier, inc=1, device_id=shifted(0, s), device_id_type=MESH)
    for w in COLUMN_PEERS:
        pl.semaphore_signal(barrier, inc=1, device_id=shifted(w, 0), device_id_type=MESH)

    to = names_in[...] >> SLOT_BITS
    to_f, to_p = to >> 4, to & 15
    dz, dc = ((to_f >> 1) - z) & 3, ((to_f & 1) - c) & 1
    dx, dy = ((to_p >> 2) - x) & 3, ((to_p & 3) - y) & 3
    step_column, step_plane = dz * 2 + dc, dx * 4 + dy
    label = step_column * PLANE + step_plane
    onehot[...] = (lax.broadcasted_iota(i32, (128, rows), 0) == label).astype(bf16)
    block = 256
    pl.semaphore_wait(barrier, PLANE + COLUMN - 2)
    for w in COLUMN_PEERS:
        pl.semaphore_signal(entered, inc=1, device_id=shifted(w, 0), device_id_type=MESH)

    upper = (
        lax.broadcasted_iota(i32, (block, block), 0) < lax.broadcasted_iota(i32, (block, block), 1)
    ).astype(bf16)
    seen = jnp.zeros((128, 1), f32)
    orders = []
    for b in range(rows // block):
        mine = onehot[:, b * block:(b + 1) * block]
        before = jnp.dot(mine, upper, preferred_element_type=f32) + seen
        wide = mine.astype(f32)
        orders.append(jnp.sum(wide * before, axis=0, keepdims=True))
        seen = seen + jnp.sum(wide, axis=1, keepdims=True)
    order = jnp.concatenate(orders, axis=1).astype(i32)
    turn = step_plane - STRIDE * step_column
    for _ in range(STRIDE * (COLUMN - 1) // (PLANE - 1) + 1):
        turn = jnp.where(turn < 1, turn + (PLANE - 1), turn)
    turn = jnp.where(step_plane == 0, 0, turn)
    position[...] = (turn * COLUMN + step_column) * CAP + order

    value = (names_in[...] & ((1 << SLOT_BITS) - 1)) + 1
    lane_order = lax.broadcasted_iota(i32, (128, rows), 0) & (CAP - 1)
    hit = lane_order == order
    nt = (((1,), (1,)), ((), ()))
    high = jnp.where(hit, (value >> 5).astype(f32), 0.0).astype(bf16)
    table = lax.dot_general(onehot[...], high, nt, preferred_element_type=f32) * 32.0
    low = jnp.where(hit, (value & 31).astype(f32), 0.0).astype(bf16)
    table = table + lax.dot_general(onehot[...], low, nt, preferred_element_type=f32)
    lane_group = lax.broadcasted_iota(i32, (128, 128), 1) >> 5
    row_group = (lax.broadcasted_iota(i32, (128, 128), 0) >> 4) & 3
    slot_out[...] = jnp.where(lane_group == row_group, table, 0.0).astype(i32)
    column_slots[0] = slot_out[0:PLANE]

    rows_copy.wait()

    def picked(rows_wanted):
        pick = (rows_wanted == position[...]).astype(bf16)
        return jnp.dot(pick, contributions[...], preferred_element_type=f32).astype(bf16)

    def build_plane(first):
        i = lax.broadcasted_iota(i32, (256, 1), 0)
        made = picked((first + (i >> 5)) * 256 + (i & 31))
        for k in range(8):
            out_rows[(first + k) * 256:(first + k) * 256 + CAP, :] = made[k * CAP:(k + 1) * CAP]

    def build(kk):
        i = lax.broadcasted_iota(i32, (256 - CAP, 1), 0)
        out_rows[pl.ds(pl.multiple_of(kk * 256 + CAP, CAP), 256 - CAP), :] = picked(kk * 256 + CAP + i)

    def row_copy(kk, w):
        at = pl.ds(pl.multiple_of(kk * 256 + w * CAP, CAP), CAP)
        return pltpu.make_async_remote_copy(
            src_ref=out_rows.at[at], dst_ref=in_rows.at[at],
            send_sem=row_send, recv_sem=row_recv.at[kk],
            device_id=shifted(w, plane_step_of(kk, w)), device_id_type=MESH,
        )

    def send_rows(first, last):
        @pl.loop(first, last)
        def _(kk):
            build(kk)
            for w in range(1, COLUMN):
                row_copy(kk, w).start()

    slot_copies = []
    for w in COLUMN_PEERS:
        copy = pltpu.make_async_remote_copy(
            src_ref=slot_out.at[pl.ds(w * PLANE, PLANE)], dst_ref=column_slots.at[w],
            send_sem=slot_send.at[w], recv_sem=slot_recv.at[w], device_id=shifted(w, 0), device_id_type=MESH,
        )
        copy.start()
        slot_copies.append(copy)

    build(0)
    for w in COLUMN_PEERS:
        row_copy(0, w).start()
    for first in (8, 0):
        build_plane(first)
        for kk in range(first, first + 8):
            if kk > 0:
                row_copy(kk, 0).start()

    pl.semaphore_wait(entered, COLUMN - 1)
    send_rows(1, 4)

    for copy in slot_copies:
        copy.wait()
    first = column_slots[0] + column_slots[1] + column_slots[2] + column_slots[3]
    second = column_slots[4] + column_slots[5] + column_slots[6] + column_slots[7]
    sub = lax.broadcasted_iota(i32, (PLANE, 8, 128), 1)
    plane_out[...] = jnp.where(sub < 4, first[:, None, :], second[:, None, :])
    plane_slots[0] = plane_out[0]
    plane_copies = []
    for s in PLANE_PEERS:
        copy = pltpu.make_async_remote_copy(
            src_ref=plane_out.at[s], dst_ref=plane_slots.at[s],
            send_sem=plane_send.at[s], recv_sem=plane_recv.at[s], device_id=shifted(0, s), device_id_type=MESH,
        )
        copy.start()
        plane_copies.append(copy)

    send_rows(4, PLANE)
    in_rows[0:CAP, :] = out_rows[0:CAP, :]

    panel_copies = []
    for s in range(PLANE):
        dx, dy = s // SIDE, s % SIDE
        owner = lax.rem(x + SIDE - dx, SIDE) * SIDE + lax.rem(y + SIDE - dy, SIDE)
        copy = pltpu.make_async_copy(
            panels.at[:, pl.ds(pl.multiple_of(owner * nodes, 128), nodes)], panel_v.at[s], panel_sem.at[s]
        )
        copy.start()
        panel_copies.append(copy)

    for copy in plane_copies:
        copy.wait()

    landed[...] = jnp.zeros_like(landed)

    def land(kk):
        group = lax.broadcasted_iota(i32, (1, 128), 1) >> 5
        parts = []
        for side in range(2):
            row = jnp.zeros((1, 128), i32)
            for k in range(4):
                w = side * 4 + k
                got = plane_slots[plane_step_of(kk, w), pl.ds(side * 4, 1), :]
                row = row + jnp.where(group == k, got, 0)
            parts.append(row)
        names = jnp.concatenate(parts, axis=1) - 1
        spread = (lax.broadcasted_iota(i32, (nodes, 256), 0) == names).astype(bf16)
        landed[...] += jnp.dot(
            spread, in_rows[pl.ds(pl.multiple_of(kk * 256, 256), 256), :], preferred_element_type=f32
        )

    def arrival(kk, start, count):
        at = pl.ds(start, count)
        return pltpu.make_async_remote_copy(
            src_ref=in_rows.at[at], dst_ref=in_rows.at[at],
            send_sem=row_send, recv_sem=row_recv.at[kk], device_id=(f, p), device_id_type=MESH,
        )

    arrival(0, CAP, 256 - CAP).wait_recv()
    land(0)

    @pl.loop(1, PLANE)
    def _(kk):
        arrival(kk, pl.multiple_of(kk * 256, 256), 256).wait_recv()
        land(kk)

    own = landed[...].astype(bf16)
    gathered[0] = own

    sent = []

    def pass_on(axis, direction, source, start, count, sem):
        dx, dy = source
        if axis == 0:
            dx = (dx + direction) % SIDE
            device = (f, lax.rem(x + direction + SIDE, SIDE) * SIDE + y)
        else:
            dy = (dy + direction) % SIDE
            device = (f, x * SIDE + lax.rem(y + direction + SIDE, SIDE))
        at = pl.ds(start, count)
        copy = pltpu.make_async_remote_copy(
            src_ref=gathered.at[source[0] * SIDE + source[1], at], dst_ref=gathered.at[dx * SIDE + dy, at],
            send_sem=gather_send, recv_sem=gather_recv.at[(dx * SIDE + dy) * 4 + sem],
            device_id=device, device_id_type=MESH,
        )
        copy.start()
        sent.append(count)

    def await_piece(source, start, count, sem):
        s = source[0] * SIDE + source[1]
        at = pl.ds(start, count)
        pltpu.make_async_remote_copy(
            src_ref=gathered.at[s, at], dst_ref=gathered.at[s, at],
            send_sem=gather_send, recv_sem=gather_recv.at[s * 4 + sem], device_id=(f, p), device_id_type=MESH,
        ).wait_recv()

    def at(lead, a, b):
        return (a, b) if lead == 0 else (b, a)

    def send_half(lead, axis, direction, source):
        pass_on(axis, direction, source, lead * half, half, lead * 2)

    def send_piece(lead, axis, direction, source, k):
        pass_on(axis, direction, source, lead * half + k * piece, piece, lead * 2 + k)

    def wait_half(lead, source):
        await_piece(source, lead * half, half, lead * 2)

    def wait_piece(lead, source, k):
        await_piece(source, lead * half + k * piece, piece, lead * 2 + k)

    def multiply(s, start, count):
        coupled[...] += jnp.dot(
            panel_v[s, :, pl.ds(start, count)], gathered[s, pl.ds(start, count), :], preferred_element_type=f32
        )

    for turned in (0, 1):
        for direction in (1, -1):
            for lead in (0, 1):
                send_half(lead, lead ^ turned, direction, (0, 0))
    traces_copy = pltpu.make_async_copy(gathered.at[0], traces, local_sem)
    traces_copy.start()
    own_t[...] = own.T
    coupled[...] = jnp.zeros_like(coupled)
    for copy in panel_copies:
        copy.wait()
    multiply(0, 0, nodes)

    def multiply_halves(places):
        for lead, place in places:
            multiply(place[0] * SIDE + place[1], lead * half, half)

    for k, a, direction in ((0, 1, 1), (1, 3, -1)):
        for lead in (0, 1):
            place = at(lead, a, 0)
            wait_half(lead, place)
            send_piece(lead, lead, direction, place, k)
            send_half(lead, 1 - lead, 1, place)
            send_half(lead, 1 - lead, -1, place)
    multiply_halves([(lead, at(lead, a, 0)) for a in (1, 3) for lead in (0, 1)])
    for k in (0, 1):
        for lead in (0, 1):
            place = at(lead, 2, 0)
            wait_piece(lead, place, k)
            send_piece(lead, 1 - lead, 1, place, k)
            send_piece(lead, 1 - lead, -1, place, k)
    for k, b, direction in ((0, 1, 1), (1, 3, -1)):
        for lead in (0, 1):
            place = at(lead, 0, b)
            wait_half(lead, place)
            send_piece(lead, 1 - lead, direction, place, k)
    multiply_halves([(lead, at(lead, a, b)) for a, b in ((2, 0), (0, 1), (0, 3)) for lead in (0, 1)])
    for a in (1, 3):
        for k, b, direction in ((0, 1, 1), (1, 3, -1)):
            for lead in (0, 1):
                place = at(lead, a, b)
                wait_half(lead, place)
                send_piece(lead, 1 - lead, direction, place, k)
        multiply_halves([(lead, at(lead, a, b)) for b in (1, 3) for lead in (0, 1)])
    for k in (0, 1):
        for lead in (0, 1):
            wait_piece(lead, at(lead, 0, 2), k)
    multiply_halves([(lead, at(lead, 0, 2)) for lead in (0, 1)])
    for lead in (0, 1):
        place = at(lead, 2, 1)
        wait_piece(lead, place, 0)
        send_piece(lead, 1 - lead, 1, place, 0)
        place = at(lead, 2, 3)
        wait_piece(lead, place, 1)
        send_piece(lead, 1 - lead, -1, place, 1)
    for lead in (0, 1):
        wait_piece(lead, at(lead, 2, 1), 1)
        wait_piece(lead, at(lead, 2, 3), 0)
    multiply_halves([(lead, at(lead, 2, b)) for b in (1, 3) for lead in (0, 1)])
    for a in (1, 3):
        for k in (0, 1):
            for lead in (0, 1):
                wait_piece(lead, at(lead, a, 2), k)
        multiply_halves([(lead, at(lead, a, 2)) for lead in (0, 1)])
    for k in (0, 1):
        for lead in (0, 1):
            wait_piece(lead, at(lead, 2, 2), k)

    last = 2 * SIDE + 2
    total = jnp.zeros((width, width), f32)
    for r in range(0, nodes, 256):
        wide = coupled[r:r + 256, :] + jnp.dot(
            panel_v[last, r:r + 256, :], gathered[last], preferred_element_type=f32
        )
        top = wide.astype(bf16)
        rest = (wide - top.astype(f32)).astype(bf16)
        left = own_t[:, r:r + 256]
        total = total + jnp.dot(left, top, preferred_element_type=f32)
        total = total + jnp.dot(left, rest, preferred_element_type=f32)
    share[...] = total
    share_sent[...] = share[...].astype(bf16)

    strip = width // PLANE
    copies = []
    for s in PLANE_PEERS:
        device = shifted(0, s)
        copy = pltpu.make_async_remote_copy(
            src_ref=share_sent.at[pl.ds(pl.multiple_of(device[1] * strip, strip), strip)], dst_ref=reduce_in.at[s],
            send_sem=reduce_send.at[s], recv_sem=reduce_recv.at[s], device_id=device, device_id_type=MESH,
        )
        copy.start()
        copies.append(copy)
    mine = pl.ds(pl.multiple_of(p * strip, strip), strip)
    total = share[mine, :]
    for copy in copies:
        copy.wait()
    for s in range(1, PLANE):
        total = total + reduce_in[s].astype(f32)
    column_in[f] = total.astype(bf16)
    copies = []
    for w in COLUMN_PEERS:
        copy = pltpu.make_async_remote_copy(
            src_ref=column_in.at[f], dst_ref=column_in.at[f],
            send_sem=column_send.at[w], recv_sem=column_recv.at[w], device_id=shifted(w, 0), device_id_type=MESH,
        )
        copy.start()
        copies.append(copy)
    for copy in copies:
        copy.wait()
    total = column_in[0].astype(f32)
    for w in range(1, COLUMN):
        total = total + column_in[w].astype(f32)
    full[mine, :] = total.astype(bf16)
    copies = []
    for s in PLANE_PEERS:
        copy = pltpu.make_async_remote_copy(
            src_ref=full.at[mine], dst_ref=full.at[mine],
            send_sem=full_send.at[s], recv_sem=full_recv.at[s], device_id=shifted(0, s), device_id_type=MESH,
        )
        copy.start()
        copies.append(copy)
    for copy in copies:
        copy.wait()
    mass[...] = full[...]
    traces_copy.wait()

    everything = pl.ds(CAP, rows * 2 - CAP)
    pltpu.make_async_remote_copy(
        src_ref=out_rows.at[everything], dst_ref=out_rows.at[everything],
        send_sem=row_send, recv_sem=row_recv.at[0], device_id=(f, p), device_id_type=MESH,
    ).wait_send()
    assert sum(sent) % nodes == 0
    blocks = pl.ds(0, sum(sent) // nodes)
    pltpu.make_async_remote_copy(
        src_ref=gathered.at[blocks], dst_ref=gathered.at[blocks],
        send_sem=gather_send, recv_sem=gather_recv.at[0], device_id=(f, p), device_id_type=MESH,
    ).wait_send()


def finish(factor, traces, summed, traces_out, mass):
    traces_out[...] = traces[...]
    wide = summed[...].astype(jnp.float32)
    mass[...] = (wide + wide.T) * factor


def shards(contributions, routes, slots, panels):
    rows, width = contributions.shape
    nodes = panels.shape[0]
    devices = lax.axis_size("fluid") * lax.axis_size("patch")
    bf16, f32, i32 = jnp.bfloat16, jnp.float32, jnp.int32
    strip = width // PLANE
    vmem, anywhere = pl.BlockSpec(memory_space=pltpu.VMEM), pl.BlockSpec(memory_space=pl.ANY)
    hbm = pl.BlockSpec(memory_space=pltpu.HBM)
    dma = pltpu.SemaphoreType.DMA
    names = (routes * (1 << SLOT_BITS) + slots.reshape(rows, 1)).reshape(1, rows)
    summed = pl.pallas_call(
        kernel,
        out_shape=(
            jax.ShapeDtypeStruct((nodes, width), bf16),
            jax.ShapeDtypeStruct((width, width), bf16),
        ),
        in_specs=[hbm, vmem, hbm],
        out_specs=(anywhere, vmem),
        scratch_shapes=[
            pltpu.VMEM((rows, width), bf16),
            pltpu.VMEM((2 * rows, width), bf16),
            pltpu.VMEM((2 * rows, width), bf16),
            pltpu.VMEM((128, rows), bf16),
            pltpu.VMEM((1, rows), i32),
            pltpu.VMEM((128, 128), i32),
            pltpu.VMEM((COLUMN, PLANE, 128), i32),
            pltpu.VMEM((PLANE, 8, 128), i32),
            pltpu.VMEM((PLANE, 8, 128), i32),
            pltpu.VMEM((nodes, width), f32),
            pltpu.VMEM((PLANE, nodes, width), bf16),
            pltpu.VMEM((PLANE, nodes, nodes), bf16),
            pltpu.VMEM((nodes, width), f32),
            pltpu.VMEM((width, nodes), bf16),
            pltpu.VMEM((width, width), f32),
            pltpu.VMEM((width, width), bf16),
            pltpu.VMEM((PLANE, strip, width), bf16),
            pltpu.VMEM((COLUMN, strip, width), bf16),
            pltpu.VMEM((width, width), bf16),
            pltpu.SemaphoreType.REGULAR,
            dma, dma((PLANE,)), dma((COLUMN,)), dma((COLUMN,)), dma((PLANE,)), dma((PLANE,)),
            dma, dma((PLANE * 4,)), dma((PLANE,)),
            dma, dma, dma((PLANE,)), dma((PLANE,)), dma((COLUMN,)), dma((COLUMN,)), dma((PLANE,)), dma((PLANE,)),
        ],
        compiler_params=pltpu.CompilerParams(
            collective_id=0, has_side_effects=True, vmem_limit_bytes=53 * 1024 * 1024
        ),
        cost_estimate=pl.CostEstimate(
            flops=2 * nodes * PLANE * nodes * width, bytes_accessed=nodes * nodes * PLANE * 2, transcendentals=0
        ),
    )(contributions, names, panels)
    return pl.pallas_call(
        functools.partial(finish, 0.5 / math.sqrt(nodes * devices)),
        out_shape=(
            jax.ShapeDtypeStruct((nodes, width), bf16),
            jax.ShapeDtypeStruct((width, width), f32),
        ),
        in_specs=[vmem, vmem],
        out_specs=(vmem, vmem),
        compiler_params=pltpu.CompilerParams(vmem_limit_bytes=4 * 1024 * 1024),
    )(*summed)


def solution(mesh):
    placed = (
        P(("fluid", "patch"), None),
        P(("fluid", "patch"), None),
        P(("fluid", "patch")),
        P(("fluid", "patch"), None),
    )
    return jax.shard_map(
        shards,
        mesh=mesh,
        in_specs=placed,
        out_specs=(P(("fluid", "patch"), None), P()),
        check_vma=False,
    )
```

```python
import functools
import math

import jax
import jax.numpy as jnp
from jax import lax
from jax.experimental import pallas as pl
from jax.experimental.pallas import tpu as pltpu
from jax.sharding import PartitionSpec as P

MESH = pl.DeviceIdType.MESH
SIDE = 4
COLUMN = 8
PLANE = 16
CAP = 32
SLOT_BITS = 10
STRIDE = 7
PLANE_PEERS = (10, 9, 11, 6, 14, 2, 8, 5, 7, 13, 15, 1, 3, 4, 12)
COLUMN_PEERS = (5, 4, 3, 7, 2, 6, 1)


def where_am_i():
    f, p = lax.axis_index("fluid"), lax.axis_index("patch")
    return f // 2, lax.rem(f, 2), p // SIDE, lax.rem(p, SIDE)


def shifted(column_step, plane_step, sign=1):
    z, c, x, y = where_am_i()
    dz, dc = column_step // 2, column_step % 2
    dx, dy = plane_step // SIDE, plane_step % SIDE
    if sign < 0:
        dz, dx, dy = SIDE - dz, SIDE - dx, SIDE - dy
    return (
        lax.rem(z + dz, SIDE) * 2 + lax.rem(c + dc, 2),
        lax.rem(x + dx, SIDE) * SIDE + lax.rem(y + dy, SIDE),
    )


def plane_step_of(turn, w):
    if isinstance(turn, int) and turn == 0:
        return 0
    return lax.rem(turn - 1 + STRIDE * w % (PLANE - 1), PLANE - 1) + 1


def kernel(
    contributions_in, names_in, panels, traces, mass,
    contributions, out_rows, in_rows, onehot, position, slot_out, column_slots, plane_out, plane_slots, landed,
    gathered, panel_v, coupled, own_t, share, share_sent, reduce_in, column_in, full, entered,
    row_send, row_recv, slot_send, slot_recv, plane_send, plane_recv, gather_send, gather_recv, panel_sem,
    operand_sem, local_sem, reduce_send, reduce_recv, column_send, column_recv, full_send, full_recv,
):
    f32, bf16, i32 = jnp.float32, jnp.bfloat16, jnp.int32
    f, p = lax.axis_index("fluid"), lax.axis_index("patch")
    z, c, x, y = where_am_i()
    rows = contributions_in.shape[0]
    nodes = traces.shape[0]
    width = traces.shape[1]
    half, piece = nodes // 2, nodes // 4

    rows_copy = pltpu.make_async_copy(contributions_in, contributions, operand_sem)
    rows_copy.start()

    barrier = pltpu.get_barrier_semaphore()

    for s in PLANE_PEERS:
        pl.semaphore_signal(barrier, inc=1, device_id=shifted(0, s), device_id_type=MESH)
    for w in COLUMN_PEERS:
        pl.semaphore_signal(barrier, inc=1, device_id=shifted(w, 0), device_id_type=MESH)

    to = names_in[...] >> SLOT_BITS
    to_f, to_p = to >> 4, to & 15
    dz, dc = ((to_f >> 1) - z) & 3, ((to_f & 1) - c) & 1
    dx, dy = ((to_p >> 2) - x) & 3, ((to_p & 3) - y) & 3
    step_column, step_plane = dz * 2 + dc, dx * 4 + dy
    label = step_column * PLANE + step_plane
    onehot[...] = (lax.broadcasted_iota(i32, (128, rows), 0) == label).astype(bf16)
    block = 256
    pl.semaphore_wait(barrier, PLANE + COLUMN - 2)
    for w in COLUMN_PEERS:
        pl.semaphore_signal(entered, inc=1, device_id=shifted(w, 0), device_id_type=MESH)

    upper = (
        lax.broadcasted_iota(i32, (block, block), 0) < lax.broadcasted_iota(i32, (block, block), 1)
    ).astype(bf16)
    seen = jnp.zeros((128, 1), f32)
    orders = []
    for b in range(rows // block):
        mine = onehot[:, b * block:(b + 1) * block]
        before = jnp.dot(mine, upper, preferred_element_type=f32) + seen
        wide = mine.astype(f32)
        orders.append(jnp.sum(wide * before, axis=0, keepdims=True))
        seen = seen + jnp.sum(wide, axis=1, keepdims=True)
    order = jnp.concatenate(orders, axis=1).astype(i32)
    turn = step_plane - STRIDE * step_column
    for _ in range(STRIDE * (COLUMN - 1) // (PLANE - 1) + 1):
        turn = jnp.where(turn < 1, turn + (PLANE - 1), turn)
    turn = jnp.where(step_plane == 0, 0, turn)
    position[...] = (turn * COLUMN + step_column) * CAP + order

    value = (names_in[...] & ((1 << SLOT_BITS) - 1)) + 1
    lane_order = lax.broadcasted_iota(i32, (128, rows), 0) & (CAP - 1)
    hit = lane_order == order
    nt = (((1,), (1,)), ((), ()))
    high = jnp.where(hit, (value >> 5).astype(f32), 0.0).astype(bf16)
    table = lax.dot_general(onehot[...], high, nt, preferred_element_type=f32) * 32.0
    low = jnp.where(hit, (value & 31).astype(f32), 0.0).astype(bf16)
    table = table + lax.dot_general(onehot[...], low, nt, preferred_element_type=f32)
    lane_group = lax.broadcasted_iota(i32, (128, 128), 1) >> 5
    row_group = (lax.broadcasted_iota(i32, (128, 128), 0) >> 4) & 3
    slot_out[...] = jnp.where(lane_group == row_group, table, 0.0).astype(i32)
    column_slots[0] = slot_out[0:PLANE]

    rows_copy.wait()

    def picked(rows_wanted):
        pick = (rows_wanted == position[...]).astype(bf16)
        return jnp.dot(pick, contributions[...], preferred_element_type=f32).astype(bf16)

    def build_plane(first):
        i = lax.broadcasted_iota(i32, (256, 1), 0)
        made = picked((first + (i >> 5)) * 256 + (i & 31))
        for k in range(8):
            out_rows[(first + k) * 256:(first + k) * 256 + CAP, :] = made[k * CAP:(k + 1) * CAP]

    def build(kk):
        i = lax.broadcasted_iota(i32, (256 - CAP, 1), 0)
        out_rows[pl.ds(pl.multiple_of(kk * 256 + CAP, CAP), 256 - CAP), :] = picked(kk * 256 + CAP + i)

    def row_copy(kk, w):
        at = pl.ds(pl.multiple_of(kk * 256 + w * CAP, CAP), CAP)
        return pltpu.make_async_remote_copy(
            src_ref=out_rows.at[at], dst_ref=in_rows.at[at],
            send_sem=row_send, recv_sem=row_recv.at[kk],
            device_id=shifted(w, plane_step_of(kk, w)), device_id_type=MESH,
        )

    def send_rows(first, last):
        @pl.loop(first, last)
        def _(kk):
            build(kk)
            for w in range(1, COLUMN):
                row_copy(kk, w).start()

    slot_copies = []
    for w in COLUMN_PEERS:
        copy = pltpu.make_async_remote_copy(
            src_ref=slot_out.at[pl.ds(w * PLANE, PLANE)], dst_ref=column_slots.at[w],
            send_sem=slot_send.at[w], recv_sem=slot_recv.at[w], device_id=shifted(w, 0), device_id_type=MESH,
        )
        copy.start()
        slot_copies.append(copy)

    build(0)
    for w in COLUMN_PEERS:
        row_copy(0, w).start()
    for first in (8, 0):
        build_plane(first)
        for kk in range(first, first + 8):
            if kk > 0:
                row_copy(kk, 0).start()

    pl.semaphore_wait(entered, COLUMN - 1)
    send_rows(1, 4)

    for copy in slot_copies:
        copy.wait()
    first = column_slots[0] + column_slots[1] + column_slots[2] + column_slots[3]
    second = column_slots[4] + column_slots[5] + column_slots[6] + column_slots[7]
    sub = lax.broadcasted_iota(i32, (PLANE, 8, 128), 1)
    plane_out[...] = jnp.where(sub < 4, first[:, None, :], second[:, None, :])
    plane_slots[0] = plane_out[0]
    plane_copies = []
    for s in PLANE_PEERS:
        copy = pltpu.make_async_remote_copy(
            src_ref=plane_out.at[s], dst_ref=plane_slots.at[s],
            send_sem=plane_send.at[s], recv_sem=plane_recv.at[s], device_id=shifted(0, s), device_id_type=MESH,
        )
        copy.start()
        plane_copies.append(copy)

    send_rows(4, PLANE)
    in_rows[0:CAP, :] = out_rows[0:CAP, :]

    panel_copies = []
    for s in range(PLANE):
        dx, dy = s // SIDE, s % SIDE
        owner = lax.rem(x + SIDE - dx, SIDE) * SIDE + lax.rem(y + SIDE - dy, SIDE)
        copy = pltpu.make_async_copy(
            panels.at[:, pl.ds(pl.multiple_of(owner * nodes, 128), nodes)], panel_v.at[s], panel_sem.at[s]
        )
        copy.start()
        panel_copies.append(copy)

    for copy in plane_copies:
        copy.wait()

    landed[...] = jnp.zeros_like(landed)

    def land(kk):
        group = lax.broadcasted_iota(i32, (1, 128), 1) >> 5
        parts = []
        for side in range(2):
            row = jnp.zeros((1, 128), i32)
            for k in range(4):
                w = side * 4 + k
                got = plane_slots[plane_step_of(kk, w), pl.ds(side * 4, 1), :]
                row = row + jnp.where(group == k, got, 0)
            parts.append(row)
        names = jnp.concatenate(parts, axis=1) - 1
        spread = (lax.broadcasted_iota(i32, (nodes, 256), 0) == names).astype(bf16)
        landed[...] += jnp.dot(
            spread, in_rows[pl.ds(pl.multiple_of(kk * 256, 256), 256), :], preferred_element_type=f32
        )

    def arrival(kk, start, count):
        at = pl.ds(start, count)
        return pltpu.make_async_remote_copy(
            src_ref=in_rows.at[at], dst_ref=in_rows.at[at],
            send_sem=row_send, recv_sem=row_recv.at[kk], device_id=(f, p), device_id_type=MESH,
        )

    arrival(0, CAP, 256 - CAP).wait_recv()
    land(0)

    @pl.loop(1, PLANE)
    def _(kk):
        arrival(kk, pl.multiple_of(kk * 256, 256), 256).wait_recv()
        land(kk)


    sent = []

    def pass_on(axis, direction, source, start, count, sem):
        dx, dy = source
        if axis == 0:
            dx = (dx + direction) % SIDE
            device = (f, lax.rem(x + direction + SIDE, SIDE) * SIDE + y)
        else:
            dy = (dy + direction) % SIDE
            device = (f, x * SIDE + lax.rem(y + direction + SIDE, SIDE))
        at = pl.ds(start, count)
        copy = pltpu.make_async_remote_copy(
            src_ref=gathered.at[source[0] * SIDE + source[1], at], dst_ref=gathered.at[dx * SIDE + dy, at],
            send_sem=gather_send, recv_sem=gather_recv.at[(dx * SIDE + dy) * 4 + sem],
            device_id=device, device_id_type=MESH,
        )
        copy.start()
        sent.append(count)

    def await_piece(source, start, count, sem):
        s = source[0] * SIDE + source[1]
        at = pl.ds(start, count)
        pltpu.make_async_remote_copy(
            src_ref=gathered.at[s, at], dst_ref=gathered.at[s, at],
            send_sem=gather_send, recv_sem=gather_recv.at[s * 4 + sem], device_id=(f, p), device_id_type=MESH,
        ).wait_recv()

    def at(lead, a, b):
        return (a, b) if lead == 0 else (b, a)

    def send_half(lead, axis, direction, source):
        pass_on(axis, direction, source, lead * half, half, lead * 2)

    def send_piece(lead, axis, direction, source, k):
        pass_on(axis, direction, source, lead * half + k * piece, piece, lead * 2 + k)

    def wait_half(lead, source):
        await_piece(source, lead * half, half, lead * 2)

    def wait_piece(lead, source, k):
        await_piece(source, lead * half + k * piece, piece, lead * 2 + k)

    def multiply(s, start, count):
        coupled[...] += jnp.dot(
            panel_v[s, :, pl.ds(start, count)], gathered[s, pl.ds(start, count), :], preferred_element_type=f32
        )

    for lead in (0, 1):
        ready = slice(lead * half, (lead + 1) * half)
        gathered[0, ready, :] = landed[ready, :].astype(bf16)
        for direction in (1, -1):
            send_half(lead, lead, direction, (0, 0))
    for direction in (1, -1):
        for lead in (0, 1):
            send_half(lead, 1 - lead, direction, (0, 0))
    traces_copy = pltpu.make_async_copy(gathered.at[0], traces, local_sem)
    traces_copy.start()
    own_t[...] = gathered[0].T
    coupled[...] = jnp.zeros_like(coupled)
    for copy in panel_copies:
        copy.wait()
    multiply(0, 0, nodes)

    def multiply_halves(places):
        for lead, place in places:
            multiply(place[0] * SIDE + place[1], lead * half, half)

    for k, a, direction in ((0, 1, 1), (1, 3, -1)):
        for lead in (0, 1):
            place = at(lead, a, 0)
            wait_half(lead, place)
            send_piece(lead, lead, direction, place, k)
            send_half(lead, 1 - lead, 1, place)
            send_half(lead, 1 - lead, -1, place)
    multiply_halves([(lead, at(lead, a, 0)) for a in (1, 3) for lead in (0, 1)])
    for k in (0, 1):
        for lead in (0, 1):
            place = at(lead, 2, 0)
            wait_piece(lead, place, k)
            send_piece(lead, 1 - lead, 1, place, k)
            send_piece(lead, 1 - lead, -1, place, k)
    for k, b, direction in ((0, 1, 1), (1, 3, -1)):
        for lead in (0, 1):
            place = at(lead, 0, b)
            wait_half(lead, place)
            send_piece(lead, 1 - lead, direction, place, k)
    multiply_halves([(lead, at(lead, a, b)) for a, b in ((2, 0), (0, 1), (0, 3)) for lead in (0, 1)])
    for a in (1, 3):
        for k, b, direction in ((0, 1, 1), (1, 3, -1)):
            for lead in (0, 1):
                place = at(lead, a, b)
                wait_half(lead, place)
                send_piece(lead, 1 - lead, direction, place, k)
        multiply_halves([(lead, at(lead, a, b)) for b in (1, 3) for lead in (0, 1)])
    for k in (0, 1):
        for lead in (0, 1):
            wait_piece(lead, at(lead, 0, 2), k)
    multiply_halves([(lead, at(lead, 0, 2)) for lead in (0, 1)])
    for lead in (0, 1):
        place = at(lead, 2, 1)
        wait_piece(lead, place, 0)
        send_piece(lead, 1 - lead, 1, place, 0)
        place = at(lead, 2, 3)
        wait_piece(lead, place, 1)
        send_piece(lead, 1 - lead, -1, place, 1)
    for lead in (0, 1):
        wait_piece(lead, at(lead, 2, 1), 1)
        wait_piece(lead, at(lead, 2, 3), 0)
    multiply_halves([(lead, at(lead, 2, b)) for b in (1, 3) for lead in (0, 1)])
    for a in (1, 3):
        for k in (0, 1):
            for lead in (0, 1):
                wait_piece(lead, at(lead, a, 2), k)
        multiply_halves([(lead, at(lead, a, 2)) for lead in (0, 1)])
    for k in (0, 1):
        for lead in (0, 1):
            wait_piece(lead, at(lead, 2, 2), k)

    last = 2 * SIDE + 2
    total = jnp.zeros((width, width), f32)
    for r in range(0, nodes, 256):
        wide = coupled[r:r + 256, :] + jnp.dot(
            panel_v[last, r:r + 256, :], gathered[last], preferred_element_type=f32
        )
        top = wide.astype(bf16)
        rest = (wide - top.astype(f32)).astype(bf16)
        left = own_t[:, r:r + 256]
        total = total + jnp.dot(left, top, preferred_element_type=f32)
        total = total + jnp.dot(left, rest, preferred_element_type=f32)
    share[...] = total
    share_sent[...] = share[...].astype(bf16)

    strip = width // PLANE
    copies = []
    for s in PLANE_PEERS:
        device = shifted(0, s)
        copy = pltpu.make_async_remote_copy(
            src_ref=share_sent.at[pl.ds(pl.multiple_of(device[1] * strip, strip), strip)], dst_ref=reduce_in.at[s],
            send_sem=reduce_send.at[s], recv_sem=reduce_recv.at[s], device_id=device, device_id_type=MESH,
        )
        copy.start()
        copies.append(copy)
    mine = pl.ds(pl.multiple_of(p * strip, strip), strip)
    total = share[mine, :]
    for copy in copies:
        copy.wait()
    for s in range(1, PLANE):
        total = total + reduce_in[s].astype(f32)
    column_in[f] = total.astype(bf16)
    copies = []
    for w in COLUMN_PEERS:
        copy = pltpu.make_async_remote_copy(
            src_ref=column_in.at[f], dst_ref=column_in.at[f],
            send_sem=column_send.at[w], recv_sem=column_recv.at[w], device_id=shifted(w, 0), device_id_type=MESH,
        )
        copy.start()
        copies.append(copy)
    for copy in copies:
        copy.wait()
    total = column_in[0].astype(f32)
    for w in range(1, COLUMN):
        total = total + column_in[w].astype(f32)
    full[mine, :] = total.astype(bf16)
    copies = []
    for s in PLANE_PEERS:
        copy = pltpu.make_async_remote_copy(
            src_ref=full.at[mine], dst_ref=full.at[mine],
            send_sem=full_send.at[s], recv_sem=full_recv.at[s], device_id=shifted(0, s), device_id_type=MESH,
        )
        copy.start()
        copies.append(copy)
    for copy in copies:
        copy.wait()
    mass[...] = full[...]
    traces_copy.wait()

    everything = pl.ds(CAP, rows * 2 - CAP)
    pltpu.make_async_remote_copy(
        src_ref=out_rows.at[everything], dst_ref=out_rows.at[everything],
        send_sem=row_send, recv_sem=row_recv.at[0], device_id=(f, p), device_id_type=MESH,
    ).wait_send()
    assert sum(sent) % nodes == 0
    blocks = pl.ds(0, sum(sent) // nodes)
    pltpu.make_async_remote_copy(
        src_ref=gathered.at[blocks], dst_ref=gathered.at[blocks],
        send_sem=gather_send, recv_sem=gather_recv.at[0], device_id=(f, p), device_id_type=MESH,
    ).wait_send()


def finish(factor, traces, summed, traces_out, mass):
    traces_out[...] = traces[...]
    wide = summed[...].astype(jnp.float32)
    mass[...] = (wide + wide.T) * factor


def shards(contributions, routes, slots, panels):
    rows, width = contributions.shape
    nodes = panels.shape[0]
    devices = lax.axis_size("fluid") * lax.axis_size("patch")
    bf16, f32, i32 = jnp.bfloat16, jnp.float32, jnp.int32
    strip = width // PLANE
    vmem, anywhere = pl.BlockSpec(memory_space=pltpu.VMEM), pl.BlockSpec(memory_space=pl.ANY)
    hbm = pl.BlockSpec(memory_space=pltpu.HBM)
    dma = pltpu.SemaphoreType.DMA
    names = (routes * (1 << SLOT_BITS) + slots.reshape(rows, 1)).reshape(1, rows)
    summed = pl.pallas_call(
        kernel,
        out_shape=(
            jax.ShapeDtypeStruct((nodes, width), bf16),
            jax.ShapeDtypeStruct((width, width), bf16),
        ),
        in_specs=[hbm, vmem, hbm],
        out_specs=(anywhere, vmem),
        scratch_shapes=[
            pltpu.VMEM((rows, width), bf16),
            pltpu.VMEM((2 * rows, width), bf16),
            pltpu.VMEM((2 * rows, width), bf16),
            pltpu.VMEM((128, rows), bf16),
            pltpu.VMEM((1, rows), i32),
            pltpu.VMEM((128, 128), i32),
            pltpu.VMEM((COLUMN, PLANE, 128), i32),
            pltpu.VMEM((PLANE, 8, 128), i32),
            pltpu.VMEM((PLANE, 8, 128), i32),
            pltpu.VMEM((nodes, width), f32),
            pltpu.VMEM((PLANE, nodes, width), bf16),
            pltpu.VMEM((PLANE, nodes, nodes), bf16),
            pltpu.VMEM((nodes, width), f32),
            pltpu.VMEM((width, nodes), bf16),
            pltpu.VMEM((width, width), f32),
            pltpu.VMEM((width, width), bf16),
            pltpu.VMEM((PLANE, strip, width), bf16),
            pltpu.VMEM((COLUMN, strip, width), bf16),
            pltpu.VMEM((width, width), bf16),
            pltpu.SemaphoreType.REGULAR,
            dma, dma((PLANE,)), dma((COLUMN,)), dma((COLUMN,)), dma((PLANE,)), dma((PLANE,)),
            dma, dma((PLANE * 4,)), dma((PLANE,)),
            dma, dma, dma((PLANE,)), dma((PLANE,)), dma((COLUMN,)), dma((COLUMN,)), dma((PLANE,)), dma((PLANE,)),
        ],
        compiler_params=pltpu.CompilerParams(
            collective_id=0, has_side_effects=True, vmem_limit_bytes=53 * 1024 * 1024
        ),
        cost_estimate=pl.CostEstimate(
            flops=2 * nodes * PLANE * nodes * width, bytes_accessed=nodes * nodes * PLANE * 2, transcendentals=0
        ),
    )(contributions, names, panels)
    return pl.pallas_call(
        functools.partial(finish, 0.5 / math.sqrt(nodes * devices)),
        out_shape=(
            jax.ShapeDtypeStruct((nodes, width), bf16),
            jax.ShapeDtypeStruct((width, width), f32),
        ),
        in_specs=[vmem, vmem],
        out_specs=(vmem, vmem),
        compiler_params=pltpu.CompilerParams(vmem_limit_bytes=4 * 1024 * 1024),
    )(*summed)


def solution(mesh):
    placed = (
        P(("fluid", "patch"), None),
        P(("fluid", "patch"), None),
        P(("fluid", "patch")),
        P(("fluid", "patch"), None),
    )
    return jax.shard_map(
        shards,
        mesh=mesh,
        in_specs=placed,
        out_specs=(P(("fluid", "patch"), None), P()),
        check_vma=False,
    )
```
